32 devices in a mesh: dom: 4 (over y, x), sub: 8 (over z, core).
Axes of the slice: x: 2, y: 2, z: 4, core: 2. Of those that a mesh axis runs over, the one named last changes fastest.
Arguments:
- coords: float32 [3, 8192], P(None, ('dom', 'sub')), may hold values from -6 to 6
- direction: float32 [3, 8192], P(None, ('dom', 'sub')), may hold values from -6 to 6
- connect: int32 [4, 32768], P(None, ('dom', 'sub')), may hold values from 0 to 383
- shape_inv: float32 [9, 32768], P(None, ('dom', 'sub')), may hold values from -3.5 to 3.5
- weight: float32 [32768], P(('dom', 'sub')), may hold values from 0.3 to 9
- send_node: int32 [32, 128], P(('dom', 'sub')), may hold values from 0 to 255
- recv_slot: int32 [32, 128], P(('dom', 'sub')), may hold values from 0 to 127, each once within a row
Outputs:
- gradient: float32 [4, 3, 8192], P(None, None, ('dom', 'sub'))
- energy: float32 [4], replicated
- min_det: float32 [4], replicated
The draws below stay inside these ranges and needn't reach their ends.
Inputs may be any that keep to these rules, and one draw needn't show every extreme that they name: `connect`: each tetrahedron's corners are local node numbers: owned nodes below 256, ghost slots above. `send_node`: owned node numbers; a node may be listed several times. `recv_slot`: each row is a permutation of the ghost slots.
All inputs are finite; a program needn't handle non-finite values.
Results may differ from the reference program's by a relative error of at most 0.0001.
Values sent between devices are 32-bit elements; how exact they have to be, the bound alone decides.
No kernel may reach another device: no remote copies, remote signals or barrier semaphores. Data moves between devices by JAX's collectives and lax.ppermute only.
A program may use at most 64 MiB of HBM per device.

```python
import math
import jax
import jax.numpy as jnp
from jax import lax

NODE_DEV = 256
TRIALS = 4
ELEM_DEV = 1024
SHARE = 32
GHOST_DEV = 128
NODES = 8192
ELEMS = 32768
N_DOM = 4
N_SUB = 8


def draw_weight(key, part):
    total_elems = ELEM_DEV * N_DOM * N_SUB
    device = (jnp.arange(total_elems) // ELEM_DEV).astype(jnp.float32)
    rising = 1.0 + 2.0 * device / max(N_DOM * N_SUB - 1, 1)
    base_value = jnp.exp(jax.random.uniform(key, (total_elems,), jnp.float32, math.log(0.5), math.log(2.0)))
    return base_value * rising


def with_ends(entries, rng, least, high):
    longest = entries.shape.index(max(entries.shape))
    spots = []
    for shift in (0, 1):
        where = [jax.random.randint(jax.random.fold_in(rng, axis), (), 0, length) for axis, length in enumerate(entries.shape)]
        where[longest] = (where[longest] + shift) % entries.shape[longest]
        spots.append(tuple(where))
    return entries.at[spots[0]].set(least).at[spots[1]].set(high)


def level_of(stream_key, shape, split, least, high):
    def one(position, shards_of):
        steps = jax.random.uniform(jax.random.fold_in(jax.random.fold_in(stream_key, 6), position), (shards_of,), jnp.float32, least / len(split), high / len(split))
        return jnp.repeat(jnp.exp(steps), shape[position] // shards_of).reshape((-1,) + (1,) * (len(shape) - position - 1))

    level = one(*split[0])
    for cut in split[1:]:
        level = level * one(*cut)
    return level


def noise(rng, dims, scale, bound, shards=(), held_as=jnp.bfloat16):
    drawn = scale * jax.random.normal(rng, dims, jnp.float32)
    if shards:
        drawn = drawn * level_of(rng, dims, shards, -0.22, 0.18)
    return jnp.clip(drawn, -bound, bound).astype(held_as)


def setup_inputs(seed: int = 0) -> dict:
    keys = jax.random.split(jax.random.key(seed), 8)
    return {
        "coords": noise(keys[0], (3, NODES), 1.0, 6.0, ((1, 32),), jnp.float32),
        "direction": noise(keys[1], (3, NODES), 0.5, 6.0, ((1, 32),), jnp.float32),
        "connect": with_ends(jax.random.randint(keys[2], (4, ELEMS), 0, NODE_DEV + GHOST_DEV), jax.random.fold_in(keys[2], 1), 0, (NODE_DEV + GHOST_DEV) - 1).astype(jnp.int32),
        "shape_inv": noise(keys[3], (9, ELEMS), 3 ** -0.5, 3.5, ((1, 32),), jnp.float32),
        "weight": draw_weight(jax.random.fold_in(keys[7], 71), 0),
        "send_node": with_ends(jax.random.randint(keys[5], (N_DOM * N_SUB, GHOST_DEV), 0, NODE_DEV), jax.random.fold_in(keys[5], 1), 0, NODE_DEV - 1).astype(jnp.int32),
        "recv_slot": jax.vmap(lambda own: jax.random.permutation(own, GHOST_DEV))(jax.random.split(keys[6], (N_DOM * N_SUB))).reshape((N_DOM * N_SUB, GHOST_DEV)).astype(jnp.int32),
    }


step_scales = (1.0, 0.5, 0.25, 0.125)

def jacobian(places, connect, shape_inv):
    elem_count = connect.shape[1]
    corners_all = jnp.take(places, connect.reshape(-1), axis=1).reshape(3, 4, elem_count)
    differ = corners_all[:, 1:] - corners_all[:, :1]
    return [[differ[row_index, 0] * shape_inv[col_index] + differ[row_index, 1] * shape_inv[3 + col_index] + differ[row_index, 2] * shape_inv[6 + col_index] for col_index in range(3)] for row_index in range(3)]

def cofactor(matrix):
    return [[matrix[1][1] * matrix[2][2] - matrix[1][2] * matrix[2][1], matrix[1][2] * matrix[2][0] - matrix[1][0] * matrix[2][2], matrix[1][0] * matrix[2][1] - matrix[1][1] * matrix[2][0]], [matrix[0][2] * matrix[2][1] - matrix[0][1] * matrix[2][2], matrix[0][0] * matrix[2][2] - matrix[0][2] * matrix[2][0], matrix[0][1] * matrix[2][0] - matrix[0][0] * matrix[2][1]], [matrix[0][1] * matrix[1][2] - matrix[0][2] * matrix[1][1], matrix[0][2] * matrix[1][0] - matrix[0][0] * matrix[1][2], matrix[0][0] * matrix[1][1] - matrix[0][1] * matrix[1][0]]]

def element_dets(places, connect, shape_inv):
    matrix = jacobian(places, connect, shape_inv)
    cofac = cofactor(matrix)
    return matrix[0][0] * cofac[0][0] + matrix[0][1] * cofac[0][1] + matrix[0][2] * cofac[0][2]

def barrier_shift(lowest):
    return lowest - 1.0 - jnp.abs(lowest)

def element_grad(places, connect, shape_inv, weight, shift, node_count):
    matrix = jacobian(places, connect, shape_inv)
    cofac = cofactor(matrix)
    determ = matrix[0][0] * cofac[0][0] + matrix[0][1] * cofac[0][1] + matrix[0][2] * cofac[0][2]
    lifted = determ - shift
    squares = matrix[0][0] * matrix[0][0]
    for row_index in range(3):
        for col_index in range(3):
            if row_index + col_index > 0:
                squares = squares + matrix[row_index][col_index] * matrix[row_index][col_index]
    power = lifted ** (-2.0 / 3.0)
    energy_part = jnp.sum(weight * squares * power) / 3.0
    scale_jac = weight * power * (2.0 / 3.0)
    scale_cof = weight * squares * power / lifted * (2.0 / 9.0)
    djac = [[scale_jac * matrix[row_index][col_index] - scale_cof * cofac[row_index][col_index] for col_index in range(3)] for row_index in range(3)]
    flat_index = connect.reshape(-1)
    rows_out = []
    for row_index in range(3):
        dedge = [djac[row_index][0] * shape_inv[3 * edge_index] + djac[row_index][1] * shape_inv[3 * edge_index + 1] + djac[row_index][2] * shape_inv[3 * edge_index + 2] for edge_index in range(3)]
        rows_out.append(jnp.concatenate([-(dedge[0] + dedge[1] + dedge[2]), dedge[0], dedge[1], dedge[2]]))
    combined = jnp.stack(rows_out)
    targets = flat_index[None, :] + node_count * jnp.arange(3, dtype=jnp.int32)[:, None]
    summed = jax.ops.segment_sum(combined.reshape(-1), targets.reshape(-1), num_segments=3 * node_count)
    return (energy_part, summed.reshape(3, node_count))

def reference(coords, direction, connect, shape_inv, weight, send_node, recv_slot):
    devices_all = N_DOM * N_SUB
    local_count = NODE_DEV + GHOST_DEV
    both = jnp.concatenate([coords, direction], axis=0).reshape(6, devices_all, NODE_DEV).transpose(1, 0, 2)
    outgoing = jax.vmap(lambda rows, picks: jnp.take(rows, picks, axis=1))(both, send_node)
    outgoing = outgoing.reshape(N_DOM, N_SUB, 6, 4, SHARE)
    arrived = jnp.stack([jnp.roll(outgoing[:, :, :, 0], 1, axis=0), jnp.roll(outgoing[:, :, :, 1], -1, axis=0), jnp.roll(outgoing[:, :, :, 2], 1, axis=1), jnp.roll(outgoing[:, :, :, 3], -1, axis=1)], axis=3)
    arrived = arrived.reshape(devices_all, 6, GHOST_DEV)
    ghosts = jax.vmap(lambda rows, slots: jnp.zeros_like(rows).at[:, slots].set(rows))(arrived, recv_slot)
    local = jnp.concatenate([both, ghosts], axis=2)

    def device_lows(device):
        local_rows = local[device]
        connect_dev = lax.dynamic_slice_in_dim(connect, device * ELEM_DEV, ELEM_DEV, 1)
        inverse_dev = lax.dynamic_slice_in_dim(shape_inv, device * ELEM_DEV, ELEM_DEV, 1)
        lows = [jnp.min(element_dets(local_rows[:3] + step_scales[trial_index] * local_rows[3:], connect_dev, inverse_dev)) for trial_index in range(TRIALS)]
        return jnp.stack(lows)
    lows = lax.map(device_lows, jnp.arange(devices_all, dtype=jnp.int32))
    lowest = lax.optimization_barrier(jnp.min(lows, axis=0))
    shifts = barrier_shift(lowest)

    def device_terms(device):
        local_rows = local[device]
        connect_dev = lax.dynamic_slice_in_dim(connect, device * ELEM_DEV, ELEM_DEV, 1)
        inverse_dev = lax.dynamic_slice_in_dim(shape_inv, device * ELEM_DEV, ELEM_DEV, 1)
        weight_dev = lax.dynamic_slice_in_dim(weight, device * ELEM_DEV, ELEM_DEV, 0)
        parts = []
        grads = []
        for trial_index in range(TRIALS):
            places = local_rows[:3] + step_scales[trial_index] * local_rows[3:]
            energy_part, grad_rows = element_grad(places, connect_dev, inverse_dev, weight_dev, shifts[trial_index], local_count)
            parts.append(energy_part)
            grads.append(grad_rows)
        return (jnp.stack(parts), jnp.stack(grads))
    parts, grads = lax.map(device_terms, jnp.arange(devices_all, dtype=jnp.int32))
    energy = lax.optimization_barrier(jnp.sum(parts, axis=0)) / (ELEM_DEV * devices_all)
    owned = grads[..., :NODE_DEV]
    ghost_grads = grads[..., NODE_DEV:]
    returned = jax.vmap(lambda rows, slots: rows[..., slots])(ghost_grads, recv_slot).reshape(N_DOM, N_SUB, TRIALS, 3, 4, SHARE)
    back_rows = jnp.stack([jnp.roll(returned[:, :, :, :, 0], -1, axis=0), jnp.roll(returned[:, :, :, :, 1], 1, axis=0), jnp.roll(returned[:, :, :, :, 2], -1, axis=1), jnp.roll(returned[:, :, :, :, 3], 1, axis=1)], axis=4)
    back_rows = back_rows.reshape(devices_all, TRIALS, 3, GHOST_DEV)
    owned = jax.vmap(lambda rows, picks, extra: rows.at[..., picks].add(extra))(owned, send_node, back_rows)
    gradient = owned.transpose(1, 2, 0, 3).reshape(TRIALS, 3, NODE_DEV * devices_all)
    return (gradient, energy, lowest)
```

```python
import functools

import jax
import jax.numpy as jnp
from jax import lax
from jax.experimental import pallas as pl
from jax.experimental.pallas import tpu as pltpu
from jax.sharding import PartitionSpec as P

TRIALS = 4
AXES = ("dom", "sub")
LANES = 128
SUBS = 8


def lane_ids():
    return lax.broadcasted_iota(jnp.int32, (SUBS, LANES), 1)


def sub_ids():
    return lax.broadcasted_iota(jnp.int32, (SUBS, LANES), 0)


def spread(row):
    return jnp.broadcast_to(row, (SUBS, LANES))


def picked(table, index):
    return jnp.take_along_axis(table, index, axis=1, mode="promise_in_bounds")


def step_lengths():
    trial = sub_ids() & (TRIALS - 1)
    return jnp.where(
        trial == 0, 1.0, jnp.where(trial == 1, 0.5, jnp.where(trial == 2, 0.25, 0.125))
    ).astype(jnp.float32)


def halves(ref, row, block, blocks):
    first = spread(ref[row : row + 1, block * LANES : (block + 1) * LANES])
    later = blocks + block
    second = spread(ref[row : row + 1, later * LANES : (later + 1) * LANES])
    return jnp.where(sub_ids() < TRIALS, first, second)


def split_three(value):
    high = value.astype(jnp.bfloat16)
    rest = value - high.astype(jnp.float32)
    mid = rest.astype(jnp.bfloat16)
    low = (rest - mid.astype(jnp.float32)).astype(jnp.bfloat16)
    return [high, mid, low]


def marks(row, count):
    places = lax.broadcasted_iota(jnp.int32, (count, row.shape[1]), 0)
    hit = places == jnp.broadcast_to(row, (count, row.shape[1]))
    return jnp.where(hit, 1.0, 0.0).astype(jnp.bfloat16)


def by_marks(left, right):
    return lax.dot_general(
        left, right, (((1,), (1,)), ((), ())), preferred_element_type=jnp.float32
    )


def send_kernel(coords, direction, send, out, table):
    table[...] = jnp.zeros_like(table)
    table[0:3, :] = coords[...]
    table[3:6, :] = direction[...]
    index = spread(send[...])
    low = index & (LANES - 1)
    first = picked(table[:, :LANES], low)
    second = picked(table[:, LANES:], low)
    out[...] = jnp.where(index < LANES, first, second)


def cofactor(m):
    return [
        [
            m[1][1] * m[2][2] - m[1][2] * m[2][1],
            m[1][2] * m[2][0] - m[1][0] * m[2][2],
            m[1][0] * m[2][1] - m[1][1] * m[2][0],
        ],
        [
            m[0][2] * m[2][1] - m[0][1] * m[2][2],
            m[0][0] * m[2][2] - m[0][2] * m[2][0],
            m[0][1] * m[2][0] - m[0][0] * m[2][1],
        ],
        [
            m[0][1] * m[1][2] - m[0][2] * m[1][1],
            m[0][2] * m[1][0] - m[0][0] * m[1][2],
            m[0][0] * m[1][1] - m[0][1] * m[1][0],
        ],
    ]


def det_kernel(
    blocks, coords, direction, got0, got1, got2, got3, connect, inverse, slots,
    low_out, jac_out, table,
):
    lane = lane_ids()
    group = lane // 32
    order = marks(slots[...], LANES)
    entry = lax.broadcasted_iota(jnp.int32, (16, LANES), 1).astype(jnp.bfloat16)
    came_at = by_marks(entry, order)[:SUBS].astype(jnp.int32)
    arrived = jnp.where(
        group == 0,
        got0[...],
        jnp.where(group == 1, got1[...], jnp.where(group == 2, got2[...], got3[...])),
    )
    ghosts = picked(arrived, came_at)
    owned = coords.shape[1]
    table[0:3, :owned] = coords[...]
    table[3:6, :owned] = direction[...]
    table[:, owned:] = ghosts
    steps = step_lengths()
    tiles = table.shape[1] // LANES
    places = [
        [
            spread(table[comp : comp + 1, tile * LANES : (tile + 1) * LANES])
            + steps * spread(table[3 + comp : 4 + comp, tile * LANES : (tile + 1) * LANES])
            for tile in range(tiles)
        ]
        for comp in range(3)
    ]
    lowest = None
    for block in range(blocks):
        corners = []
        for corner in range(4):
            index = halves(connect, corner, block, blocks)
            low = index & (LANES - 1)
            in_first = index < LANES
            in_second = index < 2 * LANES
            corners.append(
                [
                    jnp.where(
                        in_first,
                        picked(places[comp][0], low),
                        jnp.where(
                            in_second,
                            picked(places[comp][1], low),
                            picked(places[comp][2], low),
                        ),
                    )
                    for comp in range(3)
                ]
            )
        weights = [halves(inverse, row, block, blocks) for row in range(9)]
        jac = []
        for comp in range(3):
            edges = [corners[k][comp] - corners[0][comp] for k in (1, 2, 3)]
            jac.append(
                [
                    edges[0] * weights[col]
                    + edges[1] * weights[3 + col]
                    + edges[2] * weights[6 + col]
                    for col in range(3)
                ]
            )
        cofac = cofactor(jac)
        det = jac[0][0] * cofac[0][0] + jac[0][1] * cofac[0][1] + jac[0][2] * cofac[0][2]
        lowest = det if lowest is None else jnp.minimum(lowest, det)
        for comp in range(3):
            for col in range(3):
                jac_out[3 * comp + col, :, block * LANES : (block + 1) * LANES] = jac[comp][col]
    least = spread_lanes(jnp.min(lowest, axis=1, keepdims=True))
    at_trial = jnp.where(lane == (sub_ids() & (TRIALS - 1)), least, jnp.inf)
    row = jnp.min(at_trial, axis=0, keepdims=True)
    low_out[...] = jnp.broadcast_to(row, low_out.shape)


def spread_lanes(column):
    return jnp.broadcast_to(column, (SUBS, LANES))


def grad_kernel(
    blocks, sub_count, dom_count, lows, jac_in, weight, connect, inverse, slots,
    own_out, back_out, low_out,
):
    lane, sub = lane_ids(), sub_ids()
    lowest_row = jnp.min(lows[...], axis=0, keepdims=True)
    low_out[...] = lowest_row
    mine = jnp.where(lane == (sub & (TRIALS - 1)), spread(lowest_row), 0.0)
    lowest = spread_lanes(jnp.sum(mine, axis=1, keepdims=True))
    shift = lowest - 1.0 - jnp.abs(lowest)
    energy = None
    terms = [[[] for _ in range(3)] for _ in range(4)]
    for block in range(blocks):
        cut = slice(block * LANES, (block + 1) * LANES)
        jac = [[jac_in[3 * comp + col, :, cut] for col in range(3)] for comp in range(3)]
        cofac = cofactor(jac)
        det = jac[0][0] * cofac[0][0] + jac[0][1] * cofac[0][1] + jac[0][2] * cofac[0][2]
        squares = jac[0][0] * jac[0][0]
        for comp in range(3):
            for col in range(3):
                if comp + col > 0:
                    squares = squares + jac[comp][col] * jac[comp][col]
        lifted = det - shift
        power = jnp.exp(jnp.log(lifted) * (-2.0 / 3.0))
        heavy = jnp.where(
            sub < TRIALS,
            spread(weight[block : block + 1, :]),
            spread(weight[blocks + block : blocks + block + 1, :]),
        )
        scaled = heavy * power
        part = scaled * squares
        energy = part if energy is None else energy + part
        scale_jac = scaled * (2.0 / 3.0)
        scale_cof = part / lifted * (2.0 / 9.0)
        weights = [halves(inverse, row, block, blocks) for row in range(9)]
        for comp in range(3):
            djac = [scale_jac * jac[comp][col] - scale_cof * cofac[comp][col] for col in range(3)]
            edges = [
                djac[0] * weights[3 * k] + djac[1] * weights[3 * k + 1] + djac[2] * weights[3 * k + 2]
                for k in range(3)
            ]
            terms[0][comp].append(-(edges[0] + edges[1] + edges[2]))
            for k in range(3):
                terms[k + 1][comp].append(edges[k])
    width = blocks * LANES
    local = own_out.shape[1] + LANES
    sums = [None, None]
    for corner in range(4):
        values = jnp.concatenate(
            [jnp.concatenate(terms[corner][comp], axis=1) for comp in range(3)], axis=0
        )
        left = jnp.concatenate(split_three(values), axis=0)
        for half in range(2):
            row = connect[corner : corner + 1, half * width : (half + 1) * width]
            found = by_marks(left, marks(row, local))
            sums[half] = found if sums[half] is None else sums[half] + found
    rows = 3 * SUBS
    sums = [s[:rows] + s[rows : 2 * rows] + s[2 * rows :] for s in sums]
    upper = lax.broadcasted_iota(jnp.int32, (SUBS, local), 0) < TRIALS
    ghosts = []
    for comp in range(3):
        cut = slice(comp * SUBS, (comp + 1) * SUBS)
        mixed = jnp.where(upper, sums[0][cut], sums[1][cut])
        both = mixed + pltpu.roll(mixed, TRIALS, 0)
        own_out[cut, :] = both[:, : local - LANES]
        ghosts.append(picked(both[:, local - LANES :], spread(slots[...])))
    energy = spread_lanes(jnp.sum(energy, axis=1, keepdims=True))
    energy = energy + pltpu.roll(energy, TRIALS, 0)
    back_out[...] = jnp.broadcast_to(energy[None, :TRIALS], back_out.shape)
    dom, part = lax.axis_index("dom"), lax.axis_index("sub")
    targets = (
        lax.rem(dom + dom_count - 1, dom_count) * sub_count + part,
        lax.rem(dom + 1, dom_count) * sub_count + part,
        dom * sub_count + lax.rem(part + sub_count - 1, sub_count),
        dom * sub_count + lax.rem(part + 1, sub_count),
    )
    group = lane // 32
    for k in range(4):
        tile = energy
        for comp in range(3):
            turned = (32 * (comp - k)) % LANES
            moved = pltpu.roll(ghosts[comp], turned, 1) if turned else ghosts[comp]
            tile = jnp.where(group == comp, moved, tile)
        back_out[targets[k]] = tile[:TRIALS]


def final_kernel(
    sub_count, dom_count, elem_total, back, own, send, low, gradient, energy_out, low_out
):
    lane = lane_ids()[:TRIALS]
    sub = sub_ids()[:TRIALS]
    group = lane // 32
    dom, part = lax.axis_index("dom"), lax.axis_index("sub")
    sources = (
        lax.rem(dom + 1, dom_count) * sub_count + part,
        lax.rem(dom + dom_count - 1, dom_count) * sub_count + part,
        dom * sub_count + lax.rem(part + 1, sub_count),
        dom * sub_count + lax.rem(part + sub_count - 1, sub_count),
    )
    came = [back[sources[k]] for k in range(4)]
    came = [jnp.concatenate([tile, tile], axis=0) for tile in came]
    wide = lane_ids() // 32
    rows = []
    for comp in range(3):
        whole = None
        for k in range(4):
            turned = (32 * (k - comp)) % LANES
            moved = pltpu.roll(came[k], turned, 1) if turned else came[k]
            whole = moved if whole is None else jnp.where(wide == k, moved, whole)
        rows.append(whole)
    left = jnp.concatenate(split_three(jnp.concatenate(rows, axis=0)), axis=0)
    found = by_marks(left, marks(send[...], own.shape[1]))
    height = 3 * SUBS
    found = found[:height] + found[height : 2 * height] + found[2 * height :]
    found = found + own[...]
    for comp in range(3):
        gradient[:, comp, :] = found[comp * SUBS : comp * SUBS + TRIALS]
    total = jnp.sum(back[...], axis=0)
    total = jnp.broadcast_to(total[:, LANES - 1 :], (TRIALS, LANES))
    total = jnp.sum(jnp.where(lane == sub, total, 0.0), axis=0, keepdims=True)
    energy_out[...] = total[:, :TRIALS] / 3.0 / elem_total
    low_out[...] = low[:, :TRIALS]


def exchanged(tile, axis, sent_by):
    count = lax.axis_size(axis)
    return lax.ppermute(tile, axis, [(i, (i + sent_by) % count) for i in range(count)])


def per_device(coords, direction, connect, shape_inv, weight, send_node, recv_slot):
    doms, subs = lax.axis_size("dom"), lax.axis_size("sub")
    count = doms * subs
    owned = coords.shape[1]
    elems = connect.shape[1]
    blocks = elems // (2 * LANES)
    local = owned + recv_slot.shape[1]
    f32 = jnp.float32
    vmem = pltpu.CompilerParams(vmem_limit_bytes=32 * 1024 * 1024)
    outgoing = pl.pallas_call(
        send_kernel,
        out_shape=jax.ShapeDtypeStruct((SUBS, LANES), f32),
        scratch_shapes=[pltpu.VMEM((SUBS, owned), f32)],
        compiler_params=vmem,
        name="outgoing_nodes",
    )(coords, direction, send_node)
    came = (
        exchanged(outgoing, "dom", 1),
        exchanged(outgoing, "dom", -1),
        exchanged(outgoing, "sub", 1),
        exchanged(outgoing, "sub", -1),
    )
    lows, jac = pl.pallas_call(
        functools.partial(det_kernel, blocks),
        out_shape=(
            jax.ShapeDtypeStruct((count, LANES), f32),
            jax.ShapeDtypeStruct((9, SUBS, elems // 2), f32),
        ),
        scratch_shapes=[pltpu.VMEM((SUBS, local), f32)],
        compiler_params=vmem,
        name="jacobian_dets",
    )(coords, direction, *came, connect, shape_inv, recv_slot)
    lows = lax.all_to_all(lows.reshape(count, 1, LANES), AXES, 0, 0).reshape(count, LANES)
    own, back, low = pl.pallas_call(
        functools.partial(grad_kernel, blocks, subs, doms),
        out_shape=(
            jax.ShapeDtypeStruct((3 * SUBS, owned), f32),
            jax.ShapeDtypeStruct((count, TRIALS, LANES), f32),
            jax.ShapeDtypeStruct((1, LANES), f32),
        ),
        compiler_params=vmem,
        name="element_gradients",
    )(lows, jac, weight.reshape(elems // LANES, LANES), connect, shape_inv, recv_slot)
    back = lax.all_to_all(back, AXES, 0, 0)
    gradient, energy, lowest = pl.pallas_call(
        functools.partial(final_kernel, subs, doms, float(elems * count)),
        out_shape=(
            jax.ShapeDtypeStruct((TRIALS, 3, owned), f32),
            jax.ShapeDtypeStruct((1, TRIALS), f32),
            jax.ShapeDtypeStruct((1, TRIALS), f32),
        ),
        compiler_params=vmem,
        name="owner_sums",
    )(back, own, send_node, low)
    return gradient, energy.reshape(TRIALS), lowest.reshape(TRIALS)


def solution(mesh):
    placed = (
        P(None, AXES),
        P(None, AXES),
        P(None, AXES),
        P(None, AXES),
        P(AXES),
        P(AXES, None),
        P(AXES, None),
    )
    return jax.shard_map(
        per_device,
        mesh=mesh,
        in_specs=placed,
        out_specs=(P(None, None, AXES), P(), P()),
        check_vma=False,
    )
```

```python
import functools

import jax
import jax.numpy as jnp
from jax import lax
from jax.experimental import pallas as pl
from jax.experimental.pallas import tpu as pltpu
from jax.sharding import PartitionSpec as P

TRIALS = 4
AXES = ("dom", "sub")
LANES = 128
SUBS = 8


def lane_ids():
    return lax.broadcasted_iota(jnp.int32, (SUBS, LANES), 1)


def sub_ids():
    return lax.broadcasted_iota(jnp.int32, (SUBS, LANES), 0)


def spread(row):
    return jnp.broadcast_to(row, (SUBS, LANES))


def picked(table, index):
    return jnp.take_along_axis(table, index, axis=1, mode="promise_in_bounds")


def step_lengths():
    trial = sub_ids() & (TRIALS - 1)
    return jnp.where(
        trial == 0, 1.0, jnp.where(trial == 1, 0.5, jnp.where(trial == 2, 0.25, 0.125))
    ).astype(jnp.float32)


def halves(ref, row, block, blocks):
    first = spread(ref[row : row + 1, block * LANES : (block + 1) * LANES])
    later = blocks + block
    second = spread(ref[row : row + 1, later * LANES : (later + 1) * LANES])
    return jnp.where(sub_ids() < TRIALS, first, second)


def split_three(value):
    high = value.astype(jnp.bfloat16)
    rest = value - high.astype(jnp.float32)
    mid = rest.astype(jnp.bfloat16)
    low = (rest - mid.astype(jnp.float32)).astype(jnp.bfloat16)
    return [high, mid, low]


def marks(row, count):
    places = lax.broadcasted_iota(jnp.int32, (count, row.shape[1]), 0)
    hit = places == jnp.broadcast_to(row, (count, row.shape[1]))
    return jnp.where(hit, 1.0, 0.0).astype(jnp.bfloat16)


def by_marks(left, right):
    return lax.dot_general(
        left, right, (((1,), (1,)), ((), ())), preferred_element_type=jnp.float32
    )


def send_kernel(
    coords, direction, send, slots, connect, inverse, weight,
    out, table, send_out, slots_out, connect_out, inverse_out, weight_out,
    coords_in, direction_in, arrived,
):
    copies = [
        pltpu.make_async_copy(src, dst, arrived.at[i])
        for i, (src, dst) in enumerate(
            (
                (coords, coords_in),
                (direction, direction_in),
                (send, send_out),
                (slots, slots_out),
                (connect, connect_out),
                (inverse, inverse_out),
                (weight, weight_out),
            )
        )
    ]
    for copy in copies:
        copy.start()
    table[...] = jnp.zeros_like(table)
    for copy in copies[:3]:
        copy.wait()
    table[0:3, :] = coords_in[...]
    table[3:6, :] = direction_in[...]
    index = spread(send_out[...])
    low = index & (LANES - 1)
    first = picked(table[:, :LANES], low)
    second = picked(table[:, LANES:], low)
    out[...] = jnp.where(index < LANES, first, second)
    for copy in copies[3:]:
        copy.wait()


def cofactor(m):
    return [
        [
            m[1][1] * m[2][2] - m[1][2] * m[2][1],
            m[1][2] * m[2][0] - m[1][0] * m[2][2],
            m[1][0] * m[2][1] - m[1][1] * m[2][0],
        ],
        [
            m[0][2] * m[2][1] - m[0][1] * m[2][2],
            m[0][0] * m[2][2] - m[0][2] * m[2][0],
            m[0][1] * m[2][0] - m[0][0] * m[2][1],
        ],
        [
            m[0][1] * m[1][2] - m[0][2] * m[1][1],
            m[0][2] * m[1][0] - m[0][0] * m[1][2],
            m[0][0] * m[1][1] - m[0][1] * m[1][0],
        ],
    ]


def det_kernel(
    blocks, own_table, near_dom, far_dom, near_sub, far_sub, connect, inverse, slots,
    low_out, jac_out, table,
):
    lane = lane_ids()
    group = lane // 32
    order = marks(slots[...], LANES)
    entry = lax.broadcasted_iota(jnp.int32, (16, LANES), 1).astype(jnp.bfloat16)
    came_at = by_marks(entry, order)[:SUBS].astype(jnp.int32)
    from_before = group & 1
    arrived = jnp.where(
        group < 2,
        jnp.where(from_before != (lax.axis_index("dom") & 1), near_dom[...], far_dom[...]),
        jnp.where(from_before != (lax.axis_index("sub") & 1), near_sub[...], far_sub[...]),
    )
    ghosts = picked(arrived, came_at)
    owned = own_table.shape[1]
    table[:, :owned] = own_table[...]
    table[:, owned:] = ghosts
    steps = step_lengths()
    tiles = table.shape[1] // LANES
    places = [
        [
            spread(table[comp : comp + 1, tile * LANES : (tile + 1) * LANES])
            + steps * spread(table[3 + comp : 4 + comp, tile * LANES : (tile + 1) * LANES])
            for tile in range(tiles)
        ]
        for comp in range(3)
    ]
    lowest = None
    for block in range(blocks):
        corners = []
        for corner in range(4):
            index = halves(connect, corner, block, blocks)
            low = index & (LANES - 1)
            in_first = index < LANES
            in_second = index < 2 * LANES
            corners.append(
                [
                    jnp.where(
                        in_first,
                        picked(places[comp][0], low),
                        jnp.where(
                            in_second,
                            picked(places[comp][1], low),
                            picked(places[comp][2], low),
                        ),
                    )
                    for comp in range(3)
                ]
            )
        weights = [halves(inverse, row, block, blocks) for row in range(9)]
        jac = []
        for comp in range(3):
            edges = [corners[k][comp] - corners[0][comp] for k in (1, 2, 3)]
            jac.append(
                [
                    edges[0] * weights[col]
                    + edges[1] * weights[3 + col]
                    + edges[2] * weights[6 + col]
                    for col in range(3)
                ]
            )
        cofac = cofactor(jac)
        det = jac[0][0] * cofac[0][0] + jac[0][1] * cofac[0][1] + jac[0][2] * cofac[0][2]
        lowest = det if lowest is None else jnp.minimum(lowest, det)
        for comp in range(3):
            for col in range(3):
                jac_out[3 * comp + col, :, block * LANES : (block + 1) * LANES] = jac[comp][col]
    least = spread_lanes(jnp.min(lowest, axis=1, keepdims=True))
    at_trial = jnp.where(lane == (sub_ids() & (TRIALS - 1)), least, jnp.inf)
    row = jnp.min(at_trial, axis=0, keepdims=True)
    low_out[...] = jnp.broadcast_to(row, low_out.shape)


def spread_lanes(column):
    return jnp.broadcast_to(column, (SUBS, LANES))


def grad_kernel(
    blocks, sub_count, dom_count, lows, jac_in, weight, connect, inverse, slots,
    own_out, back_out, low_out,
):
    lane, sub = lane_ids(), sub_ids()
    lowest_row = jnp.min(lows[...], axis=0, keepdims=True)
    low_out[...] = lowest_row
    mine = jnp.where(lane == (sub & (TRIALS - 1)), spread(lowest_row), 0.0)
    lowest = spread_lanes(jnp.sum(mine, axis=1, keepdims=True))
    shift = lowest - 1.0 - jnp.abs(lowest)
    energy = None
    terms = [[[] for _ in range(3)] for _ in range(4)]
    for block in range(blocks):
        cut = slice(block * LANES, (block + 1) * LANES)
        jac = [[jac_in[3 * comp + col, :, cut] for col in range(3)] for comp in range(3)]
        cofac = cofactor(jac)
        det = jac[0][0] * cofac[0][0] + jac[0][1] * cofac[0][1] + jac[0][2] * cofac[0][2]
        squares = jac[0][0] * jac[0][0]
        for comp in range(3):
            for col in range(3):
                if comp + col > 0:
                    squares = squares + jac[comp][col] * jac[comp][col]
        lifted = det - shift
        power = jnp.exp(jnp.log(lifted) * (-2.0 / 3.0))
        heavy = jnp.where(
            sub < TRIALS,
            spread(weight[block : block + 1, :]),
            spread(weight[blocks + block : blocks + block + 1, :]),
        )
        scaled = heavy * power
        part = scaled * squares
        energy = part if energy is None else energy + part
        scale_jac = scaled * (2.0 / 3.0)
        scale_cof = part / lifted * (2.0 / 9.0)
        weights = [halves(inverse, row, block, blocks) for row in range(9)]
        for comp in range(3):
            djac = [scale_jac * jac[comp][col] - scale_cof * cofac[comp][col] for col in range(3)]
            edges = [
                djac[0] * weights[3 * k] + djac[1] * weights[3 * k + 1] + djac[2] * weights[3 * k + 2]
                for k in range(3)
            ]
            terms[0][comp].append(-(edges[0] + edges[1] + edges[2]))
            for k in range(3):
                terms[k + 1][comp].append(edges[k])
    width = blocks * LANES
    local = own_out.shape[1] + LANES
    sums = [None, None]
    for corner in range(4):
        values = jnp.concatenate(
            [jnp.concatenate(terms[corner][comp], axis=1) for comp in range(3)], axis=0
        )
        left = jnp.concatenate(split_three(values), axis=0)
        for half in range(2):
            row = connect[corner : corner + 1, half * width : (half + 1) * width]
            found = by_marks(left, marks(row, local))
            sums[half] = found if sums[half] is None else sums[half] + found
    rows = 3 * SUBS
    sums = [s[:rows] + s[rows : 2 * rows] + s[2 * rows :] for s in sums]
    upper = lax.broadcasted_iota(jnp.int32, (SUBS, local), 0) < TRIALS
    ghosts = []
    for comp in range(3):
        cut = slice(comp * SUBS, (comp + 1) * SUBS)
        mixed = jnp.where(upper, sums[0][cut], sums[1][cut])
        both = mixed + pltpu.roll(mixed, TRIALS, 0)
        own_out[cut, :] = both[:, : local - LANES]
        ghosts.append(picked(both[:, local - LANES :], spread(slots[...])))
    energy = spread_lanes(jnp.sum(energy, axis=1, keepdims=True))
    energy = energy + pltpu.roll(energy, TRIALS, 0)
    back_out[...] = jnp.broadcast_to(energy[None, :TRIALS], back_out.shape)
    dom, part = lax.axis_index("dom"), lax.axis_index("sub")
    targets = (
        lax.rem(dom + dom_count - 1, dom_count) * sub_count + part,
        lax.rem(dom + 1, dom_count) * sub_count + part,
        dom * sub_count + lax.rem(part + sub_count - 1, sub_count),
        dom * sub_count + lax.rem(part + 1, sub_count),
    )
    group = lane // 32
    for k in range(4):
        tile = energy
        for comp in range(3):
            turned = (32 * (comp - k)) % LANES
            moved = pltpu.roll(ghosts[comp], turned, 1) if turned else ghosts[comp]
            tile = jnp.where(group == comp, moved, tile)
        back_out[targets[k]] = tile[:TRIALS]


def final_kernel(
    sub_count, dom_count, elem_total, back, own, send, low, gradient, energy_out, low_out
):
    lane = lane_ids()[:TRIALS]
    sub = sub_ids()[:TRIALS]
    group = lane // 32
    dom, part = lax.axis_index("dom"), lax.axis_index("sub")
    sources = (
        lax.rem(dom + 1, dom_count) * sub_count + part,
        lax.rem(dom + dom_count - 1, dom_count) * sub_count + part,
        dom * sub_count + lax.rem(part + 1, sub_count),
        dom * sub_count + lax.rem(part + sub_count - 1, sub_count),
    )
    came = [back[sources[k]] for k in range(4)]
    came = [jnp.concatenate([tile, tile], axis=0) for tile in came]
    wide = lane_ids() // 32
    rows = []
    for comp in range(3):
        whole = None
        for k in range(4):
            turned = (32 * (k - comp)) % LANES
            moved = pltpu.roll(came[k], turned, 1) if turned else came[k]
            whole = moved if whole is None else jnp.where(wide == k, moved, whole)
        rows.append(whole)
    left = jnp.concatenate(split_three(jnp.concatenate(rows, axis=0)), axis=0)
    found = by_marks(left, marks(send[...], own.shape[1]))
    height = 3 * SUBS
    found = found[:height] + found[height : 2 * height] + found[2 * height :]
    found = found + own[...]
    for comp in range(3):
        gradient[comp] = found[comp * SUBS : comp * SUBS + TRIALS]
    total = jnp.sum(back[...], axis=0)
    total = jnp.broadcast_to(total[:, LANES - 1 :], (TRIALS, LANES))
    total = jnp.sum(jnp.where(lane == sub, total, 0.0), axis=0, keepdims=True)
    energy_out[...] = total[:, :TRIALS] / 3.0 / elem_total
    low_out[...] = low[:, :TRIALS]


def exchanged(tile, axis):
    count = lax.axis_size(axis)
    near = lax.ppermute(tile, axis, [(i, i ^ 1) for i in range(count)])
    far = lax.ppermute(
        tile, axis, [(i, (i + 1 if i % 2 else i - 1) % count) for i in range(count)]
    )
    return near, far


def per_device(coords, direction, connect, shape_inv, weight, send_node, recv_slot):
    doms, subs = lax.axis_size("dom"), lax.axis_size("sub")
    count = doms * subs
    owned = coords.shape[1]
    elems = connect.shape[1]
    blocks = elems // (2 * LANES)
    local = owned + recv_slot.shape[1]
    f32, i32 = jnp.float32, jnp.int32
    shaped = jax.ShapeDtypeStruct
    params = pltpu.CompilerParams(vmem_limit_bytes=32 * 1024 * 1024)
    hbm = pl.BlockSpec(memory_space=pltpu.HBM)
    outgoing, table, sends, slots, connect, inverse, heavy = pl.pallas_call(
        send_kernel,
        in_specs=[hbm] * 7,
        out_shape=(
            shaped((SUBS, LANES), f32),
            shaped((SUBS, owned), f32),
            shaped(send_node.shape, i32),
            shaped(recv_slot.shape, i32),
            shaped(connect.shape, i32),
            shaped(shape_inv.shape, f32),
            shaped((elems // LANES, LANES), f32),
        ),
        scratch_shapes=[
            pltpu.VMEM(coords.shape, f32),
            pltpu.VMEM(direction.shape, f32),
            pltpu.SemaphoreType.DMA((7,)),
        ],
        compiler_params=params,
        name="outgoing_nodes",
    )(
        *(
            pltpu.with_memory_space_constraint(given, pltpu.HBM)
            for given in (
                coords, direction, send_node, recv_slot, connect, shape_inv,
                weight.reshape(elems // LANES, LANES),
            )
        )
    )
    near_dom, far_dom = exchanged(outgoing, "dom")
    near_sub, far_sub = exchanged(outgoing, "sub")
    lows, jac = pl.pallas_call(
        functools.partial(det_kernel, blocks),
        out_shape=(
            shaped((count, LANES), f32),
            shaped((9, SUBS, elems // 2), f32),
        ),
        scratch_shapes=[pltpu.VMEM((SUBS, local), f32)],
        compiler_params=params,
        name="jacobian_dets",
    )(table, near_dom, far_dom, near_sub, far_sub, connect, inverse, slots)
    lows = lax.all_to_all(lows.reshape(count, 1, LANES), AXES, 0, 0).reshape(count, LANES)
    own, back, low = pl.pallas_call(
        functools.partial(grad_kernel, blocks, subs, doms),
        out_shape=(
            shaped((3 * SUBS, owned), f32),
            shaped((count, TRIALS, LANES), f32),
            shaped((1, LANES), f32),
        ),
        compiler_params=params,
        name="element_gradients",
    )(lows, jac, heavy, connect, inverse, slots)
    back = lax.all_to_all(back, AXES, 0, 0)
    gradient, energy, lowest = pl.pallas_call(
        functools.partial(final_kernel, subs, doms, float(elems * count)),
        out_shape=(
            shaped((3, TRIALS, owned), f32),
            shaped((1, TRIALS), f32),
            shaped((1, TRIALS), f32),
        ),
        compiler_params=params,
        name="owner_sums",
    )(back, own, sends, low)
    return gradient.transpose(1, 0, 2), energy.reshape(TRIALS), lowest.reshape(TRIALS)


def solution(mesh):
    placed = (
        P(None, AXES),
        P(None, AXES),
        P(None, AXES),
        P(None, AXES),
        P(AXES),
        P(AXES, None),
        P(AXES, None),
    )
    return jax.shard_map(
        per_device,
        mesh=mesh,
        in_specs=placed,
        out_specs=(P(None, None, AXES), P(), P()),
        check_vma=False,
    )
```

```python
import functools

import jax
import jax.numpy as jnp
from jax import lax
from jax.experimental import pallas as pl
from jax.experimental.pallas import tpu as pltpu
from jax.sharding import PartitionSpec as P

TRIALS = 4
AXES = ("dom", "sub")
LANES = 128
SUBS = 8


def lane_ids():
    return lax.broadcasted_iota(jnp.int32, (SUBS, LANES), 1)


def sub_ids():
    return lax.broadcasted_iota(jnp.int32, (SUBS, LANES), 0)


def spread(row):
    return jnp.broadcast_to(row, (SUBS, LANES))


def picked(table, index):
    return jnp.take_along_axis(table, index, axis=1, mode="promise_in_bounds")


def step_lengths():
    trial = sub_ids() & (TRIALS - 1)
    return jnp.where(
        trial == 0, 1.0, jnp.where(trial == 1, 0.5, jnp.where(trial == 2, 0.25, 0.125))
    ).astype(jnp.float32)


def halves(ref, row, block, blocks):
    first = spread(ref[row : row + 1, block * LANES : (block + 1) * LANES])
    later = blocks + block
    second = spread(ref[row : row + 1, later * LANES : (later + 1) * LANES])
    return jnp.where(sub_ids() < TRIALS, first, second)


def split_three(value):
    high = value.astype(jnp.bfloat16)
    rest = value - high.astype(jnp.float32)
    mid = rest.astype(jnp.bfloat16)
    low = (rest - mid.astype(jnp.float32)).astype(jnp.bfloat16)
    return [high, mid, low]


def marks(row, count):
    places = lax.broadcasted_iota(jnp.int32, (count, row.shape[1]), 0)
    hit = places == jnp.broadcast_to(row, (count, row.shape[1]))
    return jnp.where(hit, 1.0, 0.0).astype(jnp.bfloat16)


def column_marks(column, count):
    shape = (column.shape[0], count)
    places = lax.broadcasted_iota(jnp.int32, shape, 1)
    hit = places == jnp.broadcast_to(column, shape)
    return jnp.where(hit, 1.0, 0.0).astype(jnp.bfloat16)


def by_marks(left, right):
    return lax.dot_general(
        left, right, (((1,), (1,)), ((), ())), preferred_element_type=jnp.float32
    )


def fetch(pairs, arrived):
    copies = [
        pltpu.make_async_copy(src, dst, arrived.at[i]) for i, (src, dst) in enumerate(pairs)
    ]
    for copy in copies:
        copy.start()
    return copies


def send_kernel(
    coords, direction, send, out, table, send_out, coords_in, direction_in, arrived
):
    copies = fetch(
        ((coords, coords_in), (direction, direction_in), (send, send_out)), arrived
    )
    table[...] = jnp.zeros_like(table)
    for copy in copies:
        copy.wait()
    table[0:3, :] = coords_in[...]
    table[3:6, :] = direction_in[...]
    index = spread(send_out[...])
    low = index & (LANES - 1)
    first = picked(table[:, :LANES], low)
    second = picked(table[:, LANES:], low)
    out[...] = jnp.where(index < LANES, first, second)


def prepare_kernel(
    blocks, slots, connect, inverse, weight,
    came_out, slots_out, index_out, inverse_out, weight_out, marks_out,
    connect_in, inverse_in, weight_in, arrived,
):
    copies = fetch(
        (
            (connect, connect_in),
            (slots, slots_out),
            (weight, weight_in),
            (inverse, inverse_in),
        ),
        arrived,
    )
    copies[0].wait()
    width = blocks * LANES
    for corner in range(4):
        for block in range(blocks):
            index_out[corner, :, block * LANES : (block + 1) * LANES] = halves(
                connect_in, corner, block, blocks
            )
    nodes = marks_out.shape[2]
    for half in range(2):
        for block in range(blocks):
            start = half * width + block * LANES
            columns = jnp.transpose(
                jnp.concatenate([connect_in[:, start : start + LANES]] * 2, axis=0)
            )
            for corner in range(4):
                row = corner * width + block * LANES
                marks_out[half, row : row + LANES, :] = column_marks(
                    columns[:, corner : corner + 1], nodes
                )
    copies[1].wait()
    order = marks(slots_out[...], LANES)
    entry = lax.broadcasted_iota(jnp.int32, (16, LANES), 1).astype(jnp.bfloat16)
    came_out[...] = by_marks(entry, order)[:SUBS].astype(jnp.int32)
    copies[2].wait()
    for block in range(blocks):
        weight_out[:, block * LANES : (block + 1) * LANES] = jnp.where(
            sub_ids() < TRIALS,
            spread(weight_in[block : block + 1, :]),
            spread(weight_in[blocks + block : blocks + block + 1, :]),
        )
    copies[3].wait()
    for row in range(9):
        for block in range(blocks):
            inverse_out[row, :, block * LANES : (block + 1) * LANES] = halves(
                inverse_in, row, block, blocks
            )


def cofactor(m):
    return [
        [
            m[1][1] * m[2][2] - m[1][2] * m[2][1],
            m[1][2] * m[2][0] - m[1][0] * m[2][2],
            m[1][0] * m[2][1] - m[1][1] * m[2][0],
        ],
        [
            m[0][2] * m[2][1] - m[0][1] * m[2][2],
            m[0][0] * m[2][2] - m[0][2] * m[2][0],
            m[0][1] * m[2][0] - m[0][0] * m[2][1],
        ],
        [
            m[0][1] * m[1][2] - m[0][2] * m[1][1],
            m[0][2] * m[1][0] - m[0][0] * m[1][2],
            m[0][0] * m[1][1] - m[0][1] * m[1][0],
        ],
    ]


def det_kernel(
    blocks, orders, own_table, came3, came2, came1, came0, connect, inverse, came_at,
    low_out, jac_out, table,
):
    lane = lane_ids()
    group = lane // 32
    came = (came0, came1, came2, came3)
    near_dom, far_dom, near_sub, far_sub = (
        tile_of(kind, orders, came) for kind in ("near_dom", "far_dom", "near_sub", "far_sub")
    )
    from_before = group & 1
    arrived = jnp.where(
        group < 2,
        jnp.where(from_before != (lax.axis_index("dom") & 1), near_dom, far_dom),
        jnp.where(from_before != (lax.axis_index("sub") & 1), near_sub, far_sub),
    )
    ghosts = picked(arrived, came_at[...])
    owned = own_table.shape[1]
    table[:, :owned] = own_table[...]
    table[:, owned:] = ghosts
    steps = step_lengths()
    tiles = table.shape[1] // LANES
    places = [
        [
            spread(table[comp : comp + 1, tile * LANES : (tile + 1) * LANES])
            + steps * spread(table[3 + comp : 4 + comp, tile * LANES : (tile + 1) * LANES])
            for tile in range(tiles)
        ]
        for comp in range(3)
    ]
    lowest = None
    for block in range(blocks):
        cut = slice(block * LANES, (block + 1) * LANES)
        corners = []
        for corner in range(4):
            index = connect[corner, :, cut]
            low = index & (LANES - 1)
            in_first = index < LANES
            in_second = index < 2 * LANES
            corners.append(
                [
                    jnp.where(
                        in_first,
                        picked(places[comp][0], low),
                        jnp.where(
                            in_second,
                            picked(places[comp][1], low),
                            picked(places[comp][2], low),
                        ),
                    )
                    for comp in range(3)
                ]
            )
        weights = [inverse[row, :, cut] for row in range(9)]
        jac = []
        for comp in range(3):
            edges = [corners[k][comp] - corners[0][comp] for k in (1, 2, 3)]
            jac.append(
                [
                    edges[0] * weights[col]
                    + edges[1] * weights[3 + col]
                    + edges[2] * weights[6 + col]
                    for col in range(3)
                ]
            )
        cofac = cofactor(jac)
        det = jac[0][0] * cofac[0][0] + jac[0][1] * cofac[0][1] + jac[0][2] * cofac[0][2]
        lowest = det if lowest is None else jnp.minimum(lowest, det)
        for comp in range(3):
            for col in range(3):
                jac_out[3 * comp + col, :, cut] = jac[comp][col]
    least = spread_lanes(jnp.min(lowest, axis=1, keepdims=True))
    at_trial = jnp.where(lane == (sub_ids() & (TRIALS - 1)), least, jnp.inf)
    row = jnp.min(at_trial, axis=0, keepdims=True)
    low_out[...] = jnp.broadcast_to(row, low_out.shape)


def spread_lanes(column):
    return jnp.broadcast_to(column, (SUBS, LANES))


def grad_kernel(
    blocks, sub_count, dom_count, lows, jac_in, weight, spots, inverse, slots,
    own_out, back_out, low_out,
):
    lane, sub = lane_ids(), sub_ids()
    lowest_row = jnp.min(lows[...], axis=0, keepdims=True)
    low_out[...] = lowest_row
    lowest = picked(spread(lowest_row), sub & (TRIALS - 1))
    shift = lowest - 1.0 - jnp.abs(lowest)
    energy = None
    terms = [[[] for _ in range(3)] for _ in range(4)]
    for block in range(blocks):
        cut = slice(block * LANES, (block + 1) * LANES)
        jac = [[jac_in[3 * comp + col, :, cut] for col in range(3)] for comp in range(3)]
        cofac = cofactor(jac)
        det = jac[0][0] * cofac[0][0] + jac[0][1] * cofac[0][1] + jac[0][2] * cofac[0][2]
        squares = jac[0][0] * jac[0][0]
        for comp in range(3):
            for col in range(3):
                if comp + col > 0:
                    squares = squares + jac[comp][col] * jac[comp][col]
        lifted = det - shift
        power = jnp.exp(jnp.log(lifted) * (-2.0 / 3.0))
        heavy = weight[:, cut]
        scaled = heavy * power
        part = scaled * squares
        energy = part if energy is None else energy + part
        scale_jac = scaled * (2.0 / 3.0)
        scale_cof = part / lifted * (2.0 / 9.0)
        weights = [inverse[row, :, cut] for row in range(9)]
        for comp in range(3):
            djac = [scale_jac * jac[comp][col] - scale_cof * cofac[comp][col] for col in range(3)]
            edges = [
                djac[0] * weights[3 * k] + djac[1] * weights[3 * k + 1] + djac[2] * weights[3 * k + 2]
                for k in range(3)
            ]
            terms[0][comp].append(-(edges[0] + edges[1] + edges[2]))
            for k in range(3):
                terms[k + 1][comp].append(edges[k])
    local = own_out.shape[1] + LANES
    values = jnp.concatenate(
        [
            jnp.concatenate([part for corner in terms for part in corner[comp]], axis=1)
            for comp in range(3)
        ],
        axis=0,
    )
    left = jnp.concatenate(split_three(values), axis=0)
    sums = [
        jnp.dot(left, spots[half], preferred_element_type=jnp.float32) for half in range(2)
    ]
    rows = 3 * SUBS
    sums = [s[:rows] + s[rows : 2 * rows] + s[2 * rows :] for s in sums]
    upper = lax.broadcasted_iota(jnp.int32, (SUBS, local), 0) < TRIALS
    ghosts = []
    for comp in range(3):
        cut = slice(comp * SUBS, (comp + 1) * SUBS)
        mixed = jnp.where(upper, sums[0][cut], sums[1][cut])
        both = mixed + pltpu.roll(mixed, TRIALS, 0)
        own_out[cut, :] = both[:, : local - LANES]
        ghosts.append(picked(both[:, local - LANES :], spread(slots[...])))
    energy = spread_lanes(jnp.sum(energy, axis=1, keepdims=True))
    energy = energy + pltpu.roll(energy, TRIALS, 0)
    back_out[...] = jnp.broadcast_to(energy[None, :TRIALS], back_out.shape)
    dom, part = lax.axis_index("dom"), lax.axis_index("sub")
    targets = (
        lax.rem(dom + dom_count - 1, dom_count) * sub_count + part,
        lax.rem(dom + 1, dom_count) * sub_count + part,
        dom * sub_count + lax.rem(part + sub_count - 1, sub_count),
        dom * sub_count + lax.rem(part + 1, sub_count),
    )
    group = lane // 32
    for k in range(4):
        tile = energy
        for comp in range(3):
            turned = (32 * (comp - k)) % LANES
            moved = pltpu.roll(ghosts[comp], turned, 1) if turned else ghosts[comp]
            tile = jnp.where(group == comp, moved, tile)
        back_out[targets[k]] = tile[:TRIALS]


def final_kernel(
    sub_count, dom_count, elem_total, back, own, send, low, gradient, energy_out, low_out
):
    lane = lane_ids()[:TRIALS]
    sub = sub_ids()[:TRIALS]
    group = lane // 32
    dom, part = lax.axis_index("dom"), lax.axis_index("sub")
    sources = (
        lax.rem(dom + 1, dom_count) * sub_count + part,
        lax.rem(dom + dom_count - 1, dom_count) * sub_count + part,
        dom * sub_count + lax.rem(part + 1, sub_count),
        dom * sub_count + lax.rem(part + sub_count - 1, sub_count),
    )
    came = [back[sources[k]] for k in range(4)]
    came = [jnp.concatenate([tile, tile], axis=0) for tile in came]
    wide = lane_ids() // 32
    rows = []
    for comp in range(3):
        whole = None
        for k in range(4):
            turned = (32 * (k - comp)) % LANES
            moved = pltpu.roll(came[k], turned, 1) if turned else came[k]
            whole = moved if whole is None else jnp.where(wide == k, moved, whole)
        rows.append(whole)
    left = jnp.concatenate(split_three(jnp.concatenate(rows, axis=0)), axis=0)
    found = by_marks(left, marks(send[...], own.shape[1]))
    height = 3 * SUBS
    found = found[:height] + found[height : 2 * height] + found[2 * height :]
    found = found + own[...]
    for comp in range(3):
        gradient[comp] = found[comp * SUBS : comp * SUBS + TRIALS]
    total = jnp.sum(back[...], axis=0)
    total = jnp.broadcast_to(total[:, LANES - 1 :], (TRIALS, LANES))
    total = jnp.sum(jnp.where(lane == sub, total, 0.0), axis=0, keepdims=True)
    energy_out[...] = total[:, :TRIALS] / 3.0 / elem_total
    low_out[...] = low[:, :TRIALS]


def partner(kind, doms, subs, dom, sub):
    if kind == "near_dom":
        return (dom ^ 1) * subs + sub
    if kind == "far_dom":
        return ((dom + 1 if dom % 2 else dom - 1) % doms) * subs + sub
    if kind == "near_sub":
        return dom * subs + (sub ^ 1)
    return dom * subs + (sub + 1 if sub % 2 else sub - 1) % subs


def exchanges(subs):
    usual = ("far_dom", "far_sub", "near_dom", "near_sub")
    last = ("near_sub", "far_sub", "far_dom", "near_dom")
    return [last if sub >= subs else usual for sub in range(subs)]


def exchanged(tile, doms, subs):
    orders = exchanges(subs)
    return [
        lax.ppermute(
            tile,
            AXES,
            [
                (dom * subs + sub, partner(orders[sub][step], doms, subs, dom, sub))
                for dom in range(doms)
                for sub in range(subs)
            ],
        )
        for step in range(4)
    ]


def tile_of(kind, orders, came):
    sub = lax.axis_index("sub")
    tile = None
    for step in range(4):
        places = [place for place, order in enumerate(orders) if order[step] == kind]
        if not places:
            continue
        if tile is None:
            tile = came[step][...]
            continue
        here = functools.reduce(jnp.logical_or, [sub == place for place in places])
        tile = jnp.where(here, came[step][...], tile)
    return tile


def per_device(coords, direction, connect, shape_inv, weight, send_node, recv_slot):
    doms, subs = lax.axis_size("dom"), lax.axis_size("sub")
    count = doms * subs
    owned = coords.shape[1]
    elems = connect.shape[1]
    blocks = elems // (2 * LANES)
    local = owned + recv_slot.shape[1]
    f32, i32 = jnp.float32, jnp.int32
    shaped = jax.ShapeDtypeStruct
    params = pltpu.CompilerParams(vmem_limit_bytes=32 * 1024 * 1024)
    hbm = pl.BlockSpec(memory_space=pltpu.HBM)

    def pinned(*arrays):
        return [pltpu.with_memory_space_constraint(x, pltpu.HBM) for x in arrays]

    outgoing, table, sends = pl.pallas_call(
        send_kernel,
        in_specs=[hbm] * 3,
        out_shape=(
            shaped((SUBS, LANES), f32),
            shaped((SUBS, owned), f32),
            shaped(send_node.shape, i32),
        ),
        scratch_shapes=[
            pltpu.VMEM(coords.shape, f32),
            pltpu.VMEM(direction.shape, f32),
            pltpu.SemaphoreType.DMA((3,)),
        ],
        compiler_params=params,
        name="outgoing_nodes",
    )(*pinned(coords, direction, send_node))
    came_at, slots, index, inverse, heavy, spots = pl.pallas_call(
        functools.partial(prepare_kernel, blocks),
        in_specs=[hbm] * 4,
        out_shape=(
            shaped((SUBS, LANES), i32),
            shaped(recv_slot.shape, i32),
            shaped((4, SUBS, elems // 2), i32),
            shaped((9, SUBS, elems // 2), f32),
            shaped((SUBS, elems // 2), f32),
            shaped((2, 2 * elems, local), jnp.bfloat16),
        ),
        scratch_shapes=[
            pltpu.VMEM(connect.shape, i32),
            pltpu.VMEM(shape_inv.shape, f32),
            pltpu.VMEM((elems // LANES, LANES), f32),
            pltpu.SemaphoreType.DMA((4,)),
        ],
        compiler_params=params,
        cost_estimate=pl.CostEstimate(flops=1000000, bytes_accessed=4000000, transcendentals=0),
        name="prepared_elements",
    )(*pinned(recv_slot, connect, shape_inv, weight.reshape(elems // LANES, LANES)))
    came = exchanged(outgoing, doms, subs)
    lows, jac = pl.pallas_call(
        functools.partial(det_kernel, blocks, exchanges(subs)),
        out_shape=(
            shaped((count, LANES), f32),
            shaped((9, SUBS, elems // 2), f32),
        ),
        scratch_shapes=[pltpu.VMEM((SUBS, local), f32)],
        compiler_params=params,
        name="jacobian_dets",
    )(table, *came[::-1], index, inverse, came_at)
    lows = lax.all_to_all(lows.reshape(count, 1, LANES), AXES, 0, 0).reshape(count, LANES)
    own, back, low = pl.pallas_call(
        functools.partial(grad_kernel, blocks, subs, doms),
        out_shape=(
            shaped((3 * SUBS, owned), f32),
            shaped((count, TRIALS, LANES), f32),
            shaped((1, LANES), f32),
        ),
        compiler_params=params,
        name="element_gradients",
    )(lows, jac, heavy, spots, inverse, slots)
    back = lax.all_to_all(back, AXES, 0, 0)
    gradient, energy, lowest = pl.pallas_call(
        functools.partial(final_kernel, subs, doms, float(elems * count)),
        out_shape=(
            shaped((3, TRIALS, owned), f32),
            shaped((1, TRIALS), f32),
            shaped((1, TRIALS), f32),
        ),
        compiler_params=params,
        name="owner_sums",
    )(back, own, sends, low)
    return gradient.transpose(1, 0, 2), energy.reshape(TRIALS), lowest.reshape(TRIALS)


def solution(mesh):
    placed = (
        P(None, AXES),
        P(None, AXES),
        P(None, AXES),
        P(None, AXES),
        P(AXES),
        P(AXES, None),
        P(AXES, None),
    )
    return jax.shard_map(
        per_device,
        mesh=mesh,
        in_specs=placed,
        out_specs=(P(None, None, AXES), P(), P()),
        check_vma=False,
    )
```

```python
import functools

import jax
import jax.numpy as jnp
from jax import lax
from jax.experimental import pallas as pl
from jax.experimental.pallas import tpu as pltpu
from jax.sharding import PartitionSpec as P

TRIALS = 4
AXES = ("dom", "sub")
LANES = 128
SUBS = 8


def lane_ids():
    return lax.broadcasted_iota(jnp.int32, (SUBS, LANES), 1)


def sub_ids():
    return lax.broadcasted_iota(jnp.int32, (SUBS, LANES), 0)


def spread(row):
    return jnp.broadcast_to(row, (SUBS, LANES))


def picked(table, index):
    return jnp.take_along_axis(table, index, axis=1, mode="promise_in_bounds")


def step_lengths():
    trial = sub_ids() & (TRIALS - 1)
    return jnp.where(
        trial == 0, 1.0, jnp.where(trial == 1, 0.5, jnp.where(trial == 2, 0.25, 0.125))
    ).astype(jnp.float32)


def trial_places(table, tile, steps):
    cut = slice(tile * LANES, (tile + 1) * LANES)
    return [
        spread(table[comp : comp + 1, cut]) + steps * spread(table[3 + comp : 4 + comp, cut])
        for comp in range(3)
    ]


def halves(ref, row, block, blocks):
    first = spread(ref[row : row + 1, block * LANES : (block + 1) * LANES])
    later = blocks + block
    second = spread(ref[row : row + 1, later * LANES : (later + 1) * LANES])
    return jnp.where(sub_ids() < TRIALS, first, second)


def split_three(value):
    high = value.astype(jnp.bfloat16)
    rest = value - high.astype(jnp.float32)
    mid = rest.astype(jnp.bfloat16)
    low = (rest - mid.astype(jnp.float32)).astype(jnp.bfloat16)
    return [high, mid, low]


def marks(row, count):
    places = lax.broadcasted_iota(jnp.int32, (count, row.shape[1]), 0)
    hit = places == jnp.broadcast_to(row, (count, row.shape[1]))
    return jnp.where(hit, 1.0, 0.0).astype(jnp.bfloat16)


def column_marks(column, count):
    shape = (column.shape[0], count)
    places = lax.broadcasted_iota(jnp.int32, shape, 1)
    hit = places == jnp.broadcast_to(column, shape)
    return jnp.where(hit, 1.0, 0.0).astype(jnp.bfloat16)


def by_marks(left, right):
    return lax.dot_general(
        left, right, (((1,), (1,)), ((), ())), preferred_element_type=jnp.float32
    )


def fetch(pairs, arrived):
    copies = [
        pltpu.make_async_copy(src, dst, arrived.at[i]) for i, (src, dst) in enumerate(pairs)
    ]
    for copy in copies:
        copy.start()
    return copies


def send_kernel(
    coords, direction, send, out, table, send_out, coords_in, direction_in, arrived
):
    copies = fetch(
        ((coords, coords_in), (direction, direction_in), (send, send_out)), arrived
    )
    table[...] = jnp.zeros_like(table)
    for copy in copies:
        copy.wait()
    table[0:3, :] = coords_in[...]
    table[3:6, :] = direction_in[...]
    index = spread(send_out[...])
    low = index & (LANES - 1)
    first = picked(table[:, :LANES], low)
    second = picked(table[:, LANES:], low)
    out[...] = jnp.where(index < LANES, first, second)


def prepare_kernel(
    blocks, table, sends, slots, connect, inverse, weight,
    came_out, slots_out, index_out, corner_out, inverse_out, weight_out, marks_out,
    send_marks_out, connect_in, inverse_in, weight_in, arrived,
):
    copies = fetch(
        (
            (connect, connect_in),
            (slots, slots_out),
            (weight, weight_in),
            (inverse, inverse_in),
        ),
        arrived,
    )
    steps = step_lengths()
    firsts, seconds = trial_places(table, 0, steps), trial_places(table, 1, steps)
    columns = jnp.transpose(spread(sends[...]))
    send_marks_out[...] = column_marks(columns[:, :1], send_marks_out.shape[1])
    copies[0].wait()
    width = blocks * LANES
    for corner in range(4):
        for block in range(blocks):
            cut = slice(block * LANES, (block + 1) * LANES)
            index = halves(connect_in, corner, block, blocks)
            index_out[corner, :, cut] = index
            low = index & (LANES - 1)
            for comp in range(3):
                corner_out[3 * corner + comp, :, cut] = jnp.where(
                    index < LANES, picked(firsts[comp], low), picked(seconds[comp], low)
                )
    nodes = marks_out.shape[2]
    for half in range(2):
        for block in range(blocks):
            start = half * width + block * LANES
            columns = jnp.transpose(
                jnp.concatenate([connect_in[:, start : start + LANES]] * 2, axis=0)
            )
            for corner in range(4):
                row = (4 * block + corner) * LANES
                marks_out[half, row : row + LANES, :] = column_marks(
                    columns[:, corner : corner + 1], nodes
                )
    copies[1].wait()
    order = marks(slots_out[...], LANES)
    entry = lax.broadcasted_iota(jnp.int32, (16, LANES), 1).astype(jnp.bfloat16)
    came_out[...] = by_marks(entry, order)[:SUBS].astype(jnp.int32)
    copies[2].wait()
    for block in range(blocks):
        weight_out[:, block * LANES : (block + 1) * LANES] = jnp.where(
            sub_ids() < TRIALS,
            spread(weight_in[block : block + 1, :]),
            spread(weight_in[blocks + block : blocks + block + 1, :]),
        )
    copies[3].wait()
    for row in range(9):
        for block in range(blocks):
            inverse_out[row, :, block * LANES : (block + 1) * LANES] = halves(
                inverse_in, row, block, blocks
            )


def cofactor(m):
    return [
        [
            m[1][1] * m[2][2] - m[1][2] * m[2][1],
            m[1][2] * m[2][0] - m[1][0] * m[2][2],
            m[1][0] * m[2][1] - m[1][1] * m[2][0],
        ],
        [
            m[0][2] * m[2][1] - m[0][1] * m[2][2],
            m[0][0] * m[2][2] - m[0][2] * m[2][0],
            m[0][1] * m[2][0] - m[0][0] * m[2][1],
        ],
        [
            m[0][1] * m[1][2] - m[0][2] * m[1][1],
            m[0][2] * m[1][0] - m[0][0] * m[1][2],
            m[0][0] * m[1][1] - m[0][1] * m[1][0],
        ],
    ]


def det_kernel(
    blocks, orders, corner_in, came3, came2, came1, came0, connect, inverse, came_at,
    low_out, jac_out, table,
):
    lane = lane_ids()
    group = lane // 32
    came = (came0, came1, came2, came3)
    near_dom, far_dom, near_sub, far_sub = (
        tile_of(kind, orders, came) for kind in ("near_dom", "far_dom", "near_sub", "far_sub")
    )
    from_before = group & 1
    arrived = jnp.where(
        group < 2,
        jnp.where(from_before != (lax.axis_index("dom") & 1), near_dom, far_dom),
        jnp.where(from_before != (lax.axis_index("sub") & 1), near_sub, far_sub),
    )
    table[...] = picked(arrived, came_at[...])
    ghosts = trial_places(table, 0, step_lengths())
    owned = 2 * LANES
    lowest = None
    for block in range(blocks):
        cut = slice(block * LANES, (block + 1) * LANES)
        corners = []
        for corner in range(4):
            index = connect[corner, :, cut]
            low = index & (LANES - 1)
            corners.append(
                [
                    jnp.where(
                        index < owned,
                        corner_in[3 * corner + comp, :, cut],
                        picked(ghosts[comp], low),
                    )
                    for comp in range(3)
                ]
            )
        weights = [inverse[row, :, cut] for row in range(9)]
        jac = []
        for comp in range(3):
            edges = [corners[k][comp] - corners[0][comp] for k in (1, 2, 3)]
            jac.append(
                [
                    edges[0] * weights[col]
                    + edges[1] * weights[3 + col]
                    + edges[2] * weights[6 + col]
                    for col in range(3)
                ]
            )
        cofac = cofactor(jac)
        det = jac[0][0] * cofac[0][0] + jac[0][1] * cofac[0][1] + jac[0][2] * cofac[0][2]
        lowest = det if lowest is None else jnp.minimum(lowest, det)
        for comp in range(3):
            for col in range(3):
                jac_out[3 * comp + col, :, cut] = jac[comp][col]
    least = spread_lanes(jnp.min(lowest, axis=1, keepdims=True))
    at_trial = jnp.where(lane == (sub_ids() & (TRIALS - 1)), least, jnp.inf)
    row = jnp.min(at_trial, axis=0, keepdims=True)
    low_out[...] = jnp.broadcast_to(row, low_out.shape)


def spread_lanes(column):
    return jnp.broadcast_to(column, (SUBS, LANES))


def grad_kernel(
    blocks, sub_count, dom_count, lows, jac_in, weight, spots, inverse, slots,
    own_out, back_out, low_out,
):
    lane, sub = lane_ids(), sub_ids()
    lowest_row = jnp.min(lows[...], axis=0, keepdims=True)
    low_out[...] = lowest_row
    lowest = picked(spread(lowest_row), sub & (TRIALS - 1))
    shift = lowest - 1.0 - jnp.abs(lowest)
    energy = None
    sums = [None, None]
    for block in range(blocks):
        cut = slice(block * LANES, (block + 1) * LANES)
        jac = [[jac_in[3 * comp + col, :, cut] for col in range(3)] for comp in range(3)]
        cofac = cofactor(jac)
        det = jac[0][0] * cofac[0][0] + jac[0][1] * cofac[0][1] + jac[0][2] * cofac[0][2]
        squares = jac[0][0] * jac[0][0]
        for comp in range(3):
            for col in range(3):
                if comp + col > 0:
                    squares = squares + jac[comp][col] * jac[comp][col]
        lifted = det - shift
        power = jnp.exp(jnp.log(lifted) * (-2.0 / 3.0))
        heavy = weight[:, cut]
        scaled = heavy * power
        part = scaled * squares
        energy = part if energy is None else energy + part
        scale_jac = scaled * (2.0 / 3.0)
        scale_cof = part / lifted * (2.0 / 9.0)
        weights = [inverse[row, :, cut] for row in range(9)]
        terms = []
        for comp in range(3):
            djac = [scale_jac * jac[comp][col] - scale_cof * cofac[comp][col] for col in range(3)]
            edges = [
                djac[0] * weights[3 * k] + djac[1] * weights[3 * k + 1] + djac[2] * weights[3 * k + 2]
                for k in range(3)
            ]
            terms.append([-(edges[0] + edges[1] + edges[2]), *edges])
        values = jnp.concatenate([jnp.concatenate(parts, axis=1) for parts in terms], axis=0)
        left = jnp.concatenate(split_three(values), axis=0)
        height = 4 * LANES
        for half in range(2):
            right = spots[half, block * height : (block + 1) * height, :]
            found = jnp.dot(left, right, preferred_element_type=jnp.float32)
            sums[half] = found if block == 0 else sums[half] + found
    local = own_out.shape[1] + LANES
    rows = 3 * SUBS
    sums = [s[:rows] + s[rows : 2 * rows] + s[2 * rows :] for s in sums]
    upper = lax.broadcasted_iota(jnp.int32, (SUBS, local), 0) < TRIALS
    ghosts = []
    for comp in range(3):
        cut = slice(comp * SUBS, (comp + 1) * SUBS)
        mixed = jnp.where(upper, sums[0][cut], sums[1][cut])
        both = mixed + pltpu.roll(mixed, TRIALS, 0)
        own_out[cut, :] = both[:, : local - LANES]
        ghosts.append(picked(both[:, local - LANES :], spread(slots[...])))
    energy = spread_lanes(jnp.sum(energy, axis=1, keepdims=True))
    energy = energy + pltpu.roll(energy, TRIALS, 0)
    back_out[...] = jnp.broadcast_to(energy[None, :TRIALS], back_out.shape)
    dom, part = lax.axis_index("dom"), lax.axis_index("sub")
    targets = (
        lax.rem(dom + dom_count - 1, dom_count) * sub_count + part,
        lax.rem(dom + 1, dom_count) * sub_count + part,
        dom * sub_count + lax.rem(part + sub_count - 1, sub_count),
        dom * sub_count + lax.rem(part + 1, sub_count),
    )
    group = lane // 32
    for k in range(4):
        tile = energy
        for comp in range(3):
            turned = (32 * (comp - k)) % LANES
            moved = pltpu.roll(ghosts[comp], turned, 1) if turned else ghosts[comp]
            tile = jnp.where(group == comp, moved, tile)
        back_out[targets[k]] = tile[:TRIALS]


def final_kernel(
    sub_count, dom_count, elem_total, back, own, send_marks, low, gradient, energy_out, low_out
):
    lane = lane_ids()[:TRIALS]
    sub = sub_ids()[:TRIALS]
    group = lane // 32
    dom, part = lax.axis_index("dom"), lax.axis_index("sub")
    sources = (
        lax.rem(dom + 1, dom_count) * sub_count + part,
        lax.rem(dom + dom_count - 1, dom_count) * sub_count + part,
        dom * sub_count + lax.rem(part + 1, sub_count),
        dom * sub_count + lax.rem(part + sub_count - 1, sub_count),
    )
    came = [back[sources[k]] for k in range(4)]
    came = [jnp.concatenate([tile, tile], axis=0) for tile in came]
    wide = lane_ids() // 32
    rows = []
    for comp in range(3):
        whole = None
        for k in range(4):
            turned = (32 * (k - comp)) % LANES
            moved = pltpu.roll(came[k], turned, 1) if turned else came[k]
            whole = moved if whole is None else jnp.where(wide == k, moved, whole)
        rows.append(whole)
    left = jnp.concatenate(split_three(jnp.concatenate(rows, axis=0)), axis=0)
    found = jnp.dot(left, send_marks[...], preferred_element_type=jnp.float32)
    height = 3 * SUBS
    found = found[:height] + found[height : 2 * height] + found[2 * height :]
    found = found + own[...]
    for comp in range(3):
        gradient[comp] = found[comp * SUBS : comp * SUBS + TRIALS]
    total = jnp.sum(back[...], axis=0)
    total = jnp.broadcast_to(total[:, LANES - 1 :], (TRIALS, LANES))
    total = jnp.sum(jnp.where(lane == sub, total, 0.0), axis=0, keepdims=True)
    energy_out[...] = total[:, :TRIALS] / 3.0 / elem_total
    low_out[...] = low[:, :TRIALS]


def partner(kind, doms, subs, dom, sub):
    if kind == "near_dom":
        return (dom ^ 1) * subs + sub
    if kind == "far_dom":
        return ((dom + 1 if dom % 2 else dom - 1) % doms) * subs + sub
    if kind == "near_sub":
        return dom * subs + (sub ^ 1)
    return dom * subs + (sub + 1 if sub % 2 else sub - 1) % subs


def exchanges(subs):
    usual = ("far_dom", "far_sub", "near_dom", "near_sub")
    last = ("near_sub", "far_sub", "far_dom", "near_dom")
    return [last if sub >= subs else usual for sub in range(subs)]


def exchanged(tile, doms, subs):
    orders = exchanges(subs)
    return [
        lax.ppermute(
            tile,
            AXES,
            [
                (dom * subs + sub, partner(orders[sub][step], doms, subs, dom, sub))
                for dom in range(doms)
                for sub in range(subs)
            ],
        )
        for step in range(4)
    ]


def tile_of(kind, orders, came):
    sub = lax.axis_index("sub")
    tile = None
    for step in range(4):
        places = [place for place, order in enumerate(orders) if order[step] == kind]
        if not places:
            continue
        if tile is None:
            tile = came[step][...]
            continue
        here = functools.reduce(jnp.logical_or, [sub == place for place in places])
        tile = jnp.where(here, came[step][...], tile)
    return tile


def per_device(coords, direction, connect, shape_inv, weight, send_node, recv_slot):
    doms, subs = lax.axis_size("dom"), lax.axis_size("sub")
    count = doms * subs
    owned = coords.shape[1]
    elems = connect.shape[1]
    blocks = elems // (2 * LANES)
    local = owned + recv_slot.shape[1]
    f32, i32 = jnp.float32, jnp.int32
    shaped = jax.ShapeDtypeStruct
    params = pltpu.CompilerParams(vmem_limit_bytes=32 * 1024 * 1024)
    hbm = pl.BlockSpec(memory_space=pltpu.HBM)

    def pinned(*arrays):
        return [pltpu.with_memory_space_constraint(x, pltpu.HBM) for x in arrays]

    outgoing, table, sends = pl.pallas_call(
        send_kernel,
        in_specs=[hbm] * 3,
        out_shape=(
            shaped((SUBS, LANES), f32),
            shaped((SUBS, owned), f32),
            shaped(send_node.shape, i32),
        ),
        scratch_shapes=[
            pltpu.VMEM(coords.shape, f32),
            pltpu.VMEM(direction.shape, f32),
            pltpu.SemaphoreType.DMA((3,)),
        ],
        compiler_params=params,
        name="outgoing_nodes",
    )(*pinned(coords, direction, send_node))
    came_at, slots, index, corners, inverse, heavy, spots, send_marks = pl.pallas_call(
        functools.partial(prepare_kernel, blocks),
        in_specs=[pl.BlockSpec(memory_space=pltpu.VMEM)] * 2 + [hbm] * 4,
        out_shape=(
            shaped((SUBS, LANES), i32),
            shaped(recv_slot.shape, i32),
            shaped((4, SUBS, elems // 2), i32),
            shaped((12, SUBS, elems // 2), f32),
            shaped((9, SUBS, elems // 2), f32),
            shaped((SUBS, elems // 2), f32),
            shaped((2, 2 * elems, local), jnp.bfloat16),
            shaped((LANES, owned), jnp.bfloat16),
        ),
        scratch_shapes=[
            pltpu.VMEM(connect.shape, i32),
            pltpu.VMEM(shape_inv.shape, f32),
            pltpu.VMEM((elems // LANES, LANES), f32),
            pltpu.SemaphoreType.DMA((4,)),
        ],
        compiler_params=params,
        cost_estimate=pl.CostEstimate(flops=1000000, bytes_accessed=4000000, transcendentals=0),
        name="prepared_elements",
    )(
        table, sends,
        *pinned(recv_slot, connect, shape_inv, weight.reshape(elems // LANES, LANES)),
    )
    came = exchanged(outgoing, doms, subs)
    lows, jac = pl.pallas_call(
        functools.partial(det_kernel, blocks, exchanges(subs)),
        out_shape=(
            shaped((count, LANES), f32),
            shaped((9, SUBS, elems // 2), f32),
        ),
        scratch_shapes=[pltpu.VMEM((SUBS, LANES), f32)],
        compiler_params=params,
        name="jacobian_dets",
    )(corners, *came[::-1], index, inverse, came_at)
    lows = lax.all_to_all(lows.reshape(count, 1, LANES), AXES, 0, 0).reshape(count, LANES)
    own, back, low = pl.pallas_call(
        functools.partial(grad_kernel, blocks, subs, doms),
        out_shape=(
            shaped((3 * SUBS, owned), f32),
            shaped((count, TRIALS, LANES), f32),
            shaped((1, LANES), f32),
        ),
        compiler_params=params,
        name="element_gradients",
    )(lows, jac, heavy, spots, inverse, slots)
    back = lax.all_to_all(back, AXES, 0, 0)
    gradient, energy, lowest = pl.pallas_call(
        functools.partial(final_kernel, subs, doms, float(elems * count)),
        out_shape=(
            shaped((3, TRIALS, owned), f32),
            shaped((1, TRIALS), f32),
            shaped((1, TRIALS), f32),
        ),
        compiler_params=params,
        name="owner_sums",
    )(back, own, send_marks, low)
    return gradient.transpose(1, 0, 2), energy.reshape(TRIALS), lowest.reshape(TRIALS)


def solution(mesh):
    placed = (
        P(None, AXES),
        P(None, AXES),
        P(None, AXES),
        P(None, AXES),
        P(AXES),
        P(AXES, None),
        P(AXES, None),
    )
    return jax.shard_map(
        per_device,
        mesh=mesh,
        in_specs=placed,
        out_specs=(P(None, None, AXES), P(), P()),
        check_vma=False,
    )
```

```python
import functools

import jax
import jax.numpy as jnp
from jax import lax
from jax.experimental import pallas as pl
from jax.experimental.pallas import tpu as pltpu
from jax.sharding import PartitionSpec as P

TRIALS = 4
AXES = ("dom", "sub")
LANES = 128
SHARE = 32
SUBS = 8


def lane_ids():
    return lax.broadcasted_iota(jnp.int32, (SUBS, LANES), 1)


def sub_ids():
    return lax.broadcasted_iota(jnp.int32, (SUBS, LANES), 0)


def spread(row):
    return jnp.broadcast_to(row, (SUBS, LANES))


def picked(table, index):
    return jnp.take_along_axis(table, index, axis=1, mode="promise_in_bounds")


def step_lengths():
    trial = sub_ids() & (TRIALS - 1)
    return jnp.where(
        trial == 0, 1.0, jnp.where(trial == 1, 0.5, jnp.where(trial == 2, 0.25, 0.125))
    ).astype(jnp.float32)


def trial_places(table, tile, steps):
    cut = slice(tile * LANES, (tile + 1) * LANES)
    return [
        spread(table[comp : comp + 1, cut]) + steps * spread(table[3 + comp : 4 + comp, cut])
        for comp in range(3)
    ]


def halves(ref, row, block, blocks):
    first = spread(ref[row : row + 1, block * LANES : (block + 1) * LANES])
    later = blocks + block
    second = spread(ref[row : row + 1, later * LANES : (later + 1) * LANES])
    return jnp.where(sub_ids() < TRIALS, first, second)


def split_three(value):
    high = value.astype(jnp.bfloat16)
    rest = value - high.astype(jnp.float32)
    mid = rest.astype(jnp.bfloat16)
    low = (rest - mid.astype(jnp.float32)).astype(jnp.bfloat16)
    return [high, mid, low]


def marks(row, count):
    places = lax.broadcasted_iota(jnp.int32, (count, row.shape[1]), 0)
    hit = places == jnp.broadcast_to(row, (count, row.shape[1]))
    return jnp.where(hit, 1.0, 0.0).astype(jnp.bfloat16)


def column_marks(column, count):
    shape = (column.shape[0], count)
    places = lax.broadcasted_iota(jnp.int32, shape, 1)
    hit = places == jnp.broadcast_to(column, shape)
    return jnp.where(hit, 1.0, 0.0).astype(jnp.bfloat16)


def by_marks(left, right):
    return lax.dot_general(
        left, right, (((1,), (1,)), ((), ())), preferred_element_type=jnp.float32
    )


def fetch(pairs, arrived):
    copies = [
        pltpu.make_async_copy(src, dst, arrived.at[i]) for i, (src, dst) in enumerate(pairs)
    ]
    for copy in copies:
        copy.start()
    return copies


def send_kernel(
    coords, direction, send, slots, connect,
    out, table, send_out, slots_out, connect_out, coords_in, direction_in, arrived,
):
    copies = fetch(
        (
            (coords, coords_in),
            (direction, direction_in),
            (send, send_out),
            (slots, slots_out),
            (connect, connect_out),
        ),
        arrived,
    )
    table[...] = jnp.zeros_like(table)
    for copy in copies[:3]:
        copy.wait()
    table[0:3, :] = coords_in[...]
    table[3:6, :] = direction_in[...]
    index = spread(send_out[...])
    low = index & (LANES - 1)
    first = picked(table[:, :LANES], low)
    second = picked(table[:, LANES:], low)
    out[...] = jnp.where(index < LANES, first, second)
    for copy in copies[3:]:
        copy.wait()


def prepare_kernel(
    blocks, table, sends, slots_in, connect_in, inverse, weight,
    index_out, corner_out, inverse_out, weight_out, marks_out, send_marks_out,
    inverse_in, weight_in, arrived,
):
    copies = fetch(((weight, weight_in), (inverse, inverse_in)), arrived)
    steps = step_lengths()
    firsts, seconds = trial_places(table, 0, steps), trial_places(table, 1, steps)
    owned = table.shape[1]
    nodes = marks_out.shape[2]
    order = marks(slots_in[...], LANES)
    entry = lax.broadcasted_iota(jnp.int32, (16, LANES), 1).astype(jnp.bfloat16)
    came_at = by_marks(entry, order)[:SUBS].astype(jnp.int32)

    def renumbered(given):
        moved = owned + picked(came_at, given & (LANES - 1))
        return jnp.where(given < owned, given, moved)

    for block in range(blocks):
        cut = slice(block * LANES, (block + 1) * LANES)
        for corner in range(4):
            index = halves(connect_in, corner, block, blocks)
            low = index & (LANES - 1)
            for comp in range(3):
                corner_out[3 * corner + comp, :, cut] = jnp.where(
                    index < LANES, picked(firsts[comp], low), picked(seconds[comp], low)
                )
            index_out[corner, :, cut] = renumbered(index)
    columns = jnp.transpose(spread(sends[...]))
    send_marks_out[...] = column_marks(columns[:, :1], send_marks_out.shape[1])
    for block in range(2 * blocks):
        given = connect_in[:, block * LANES : (block + 1) * LANES]
        columns = jnp.transpose(renumbered(jnp.concatenate([given, given], axis=0)))
        half, place = block // blocks, block % blocks
        for corner in range(4):
            row = (4 * place + corner) * LANES
            marks_out[half, row : row + LANES, :] = column_marks(
                columns[:, corner : corner + 1], nodes
            )
    for copy in copies:
        copy.wait()
    for block in range(blocks):
        cut = slice(block * LANES, (block + 1) * LANES)
        weight_out[:, cut] = jnp.where(
            sub_ids() < TRIALS,
            spread(weight_in[block : block + 1, :]),
            spread(weight_in[blocks + block : blocks + block + 1, :]),
        )
        for row in range(9):
            inverse_out[row, :, cut] = halves(inverse_in, row, block, blocks)


def cofactor(m):
    return [
        [
            m[1][1] * m[2][2] - m[1][2] * m[2][1],
            m[1][2] * m[2][0] - m[1][0] * m[2][2],
            m[1][0] * m[2][1] - m[1][1] * m[2][0],
        ],
        [
            m[0][2] * m[2][1] - m[0][1] * m[2][2],
            m[0][0] * m[2][2] - m[0][2] * m[2][0],
            m[0][1] * m[2][0] - m[0][0] * m[2][1],
        ],
        [
            m[0][1] * m[1][2] - m[0][2] * m[1][1],
            m[0][2] * m[1][0] - m[0][0] * m[1][2],
            m[0][0] * m[1][1] - m[0][1] * m[1][0],
        ],
    ]


def det_kernel(
    blocks, owned, corner_in, near_sub, near_dom, far_sub, far_dom, connect, inverse,
    low_out, jac_out, table,
):
    lane = lane_ids()
    group = lane // SHARE
    from_before = group & 1
    table[...] = jnp.where(
        group < 2,
        jnp.where(from_before != (lax.axis_index("dom") & 1), near_dom[...], far_dom[...]),
        jnp.where(from_before != (lax.axis_index("sub") & 1), near_sub[...], far_sub[...]),
    )
    ghosts = trial_places(table, 0, step_lengths())
    lowest = None
    for block in range(blocks):
        cut = slice(block * LANES, (block + 1) * LANES)
        corners = []
        for corner in range(4):
            index = connect[corner, :, cut]
            low = index & (LANES - 1)
            corners.append(
                [
                    jnp.where(
                        index < owned,
                        corner_in[3 * corner + comp, :, cut],
                        picked(ghosts[comp], low),
                    )
                    for comp in range(3)
                ]
            )
        weights = [inverse[row, :, cut] for row in range(9)]
        jac = []
        for comp in range(3):
            edges = [corners[k][comp] - corners[0][comp] for k in (1, 2, 3)]
            jac.append(
                [
                    edges[0] * weights[col]
                    + edges[1] * weights[3 + col]
                    + edges[2] * weights[6 + col]
                    for col in range(3)
                ]
            )
        cofac = cofactor(jac)
        det = jac[0][0] * cofac[0][0] + jac[0][1] * cofac[0][1] + jac[0][2] * cofac[0][2]
        lowest = det if lowest is None else jnp.minimum(lowest, det)
        for comp in range(3):
            for col in range(3):
                jac_out[3 * comp + col, :, cut] = jac[comp][col]
    least = spread_lanes(jnp.min(lowest, axis=1, keepdims=True))
    at_trial = jnp.where(lane == (sub_ids() & (TRIALS - 1)), least, jnp.inf)
    row = jnp.min(at_trial, axis=0, keepdims=True)
    low_out[...] = jnp.broadcast_to(row, low_out.shape)


def spread_lanes(column):
    return jnp.broadcast_to(column, (SUBS, LANES))


def grad_kernel(
    blocks, sub_count, dom_count, lows, jac_in, weight, spots, inverse,
    own_out, back_out, low_out,
):
    lane, sub = lane_ids(), sub_ids()
    lowest_row = jnp.min(lows[...], axis=0, keepdims=True)
    low_out[...] = lowest_row
    lowest = picked(spread(lowest_row), sub & (TRIALS - 1))
    shift = lowest - 1.0 - jnp.abs(lowest)
    energy = None
    sums = [None, None]
    for block in range(blocks):
        cut = slice(block * LANES, (block + 1) * LANES)
        jac = [[jac_in[3 * comp + col, :, cut] for col in range(3)] for comp in range(3)]
        cofac = cofactor(jac)
        det = jac[0][0] * cofac[0][0] + jac[0][1] * cofac[0][1] + jac[0][2] * cofac[0][2]
        squares = jac[0][0] * jac[0][0]
        for comp in range(3):
            for col in range(3):
                if comp + col > 0:
                    squares = squares + jac[comp][col] * jac[comp][col]
        lifted = det - shift
        power = jnp.exp(jnp.log(lifted) * (-2.0 / 3.0))
        heavy = weight[:, cut]
        scaled = heavy * power
        part = scaled * squares
        energy = part if energy is None else energy + part
        scale_jac = scaled * (2.0 / 3.0)
        scale_cof = part / lifted * (2.0 / 9.0)
        weights = [inverse[row, :, cut] for row in range(9)]
        terms = []
        for comp in range(3):
            djac = [scale_jac * jac[comp][col] - scale_cof * cofac[comp][col] for col in range(3)]
            edges = [
                djac[0] * weights[3 * k] + djac[1] * weights[3 * k + 1] + djac[2] * weights[3 * k + 2]
                for k in range(3)
            ]
            terms.append([-(edges[0] + edges[1] + edges[2]), *edges])
        values = jnp.concatenate([jnp.concatenate(parts, axis=1) for parts in terms], axis=0)
        left = jnp.concatenate(split_three(values), axis=0)
        height = 4 * LANES
        for half in range(2):
            right = spots[half, block * height : (block + 1) * height, :]
            found = jnp.dot(left, right, preferred_element_type=jnp.float32)
            sums[half] = found if block == 0 else sums[half] + found
    local = own_out.shape[1] + LANES
    rows = 3 * SUBS
    sums = [s[:rows] + s[rows : 2 * rows] + s[2 * rows :] for s in sums]
    upper = lax.broadcasted_iota(jnp.int32, (SUBS, local), 0) < TRIALS
    ghosts = []
    for comp in range(3):
        cut = slice(comp * SUBS, (comp + 1) * SUBS)
        mixed = jnp.where(upper, sums[0][cut], sums[1][cut])
        both = mixed + pltpu.roll(mixed, TRIALS, 0)
        own_out[cut, :] = both[:, : local - LANES]
        ghosts.append(both[:, local - LANES :])
    energy = spread_lanes(jnp.sum(energy, axis=1, keepdims=True))
    energy = energy + pltpu.roll(energy, TRIALS, 0)
    back_out[...] = jnp.broadcast_to(energy[None, :TRIALS], back_out.shape)
    dom, part = lax.axis_index("dom"), lax.axis_index("sub")
    targets = (
        lax.rem(dom + dom_count - 1, dom_count) * sub_count + part,
        lax.rem(dom + 1, dom_count) * sub_count + part,
        dom * sub_count + lax.rem(part + sub_count - 1, sub_count),
        dom * sub_count + lax.rem(part + 1, sub_count),
    )
    group = lane // SHARE
    for k in range(4):
        tile = energy
        for comp in range(3):
            turned = (SHARE * (comp - k)) % LANES
            moved = pltpu.roll(ghosts[comp], turned, 1) if turned else ghosts[comp]
            tile = jnp.where(group == comp, moved, tile)
        back_out[targets[k]] = tile[:TRIALS]


def final_kernel(
    sub_count, dom_count, elem_total, back, own, send_marks, low, gradient, energy_out, low_out
):
    lane = lane_ids()[:TRIALS]
    sub = sub_ids()[:TRIALS]
    group = lane // SHARE
    dom, part = lax.axis_index("dom"), lax.axis_index("sub")
    sources = (
        lax.rem(dom + 1, dom_count) * sub_count + part,
        lax.rem(dom + dom_count - 1, dom_count) * sub_count + part,
        dom * sub_count + lax.rem(part + 1, sub_count),
        dom * sub_count + lax.rem(part + sub_count - 1, sub_count),
    )
    came = [back[sources[k]] for k in range(4)]
    came = [jnp.concatenate([tile, tile], axis=0) for tile in came]
    wide = lane_ids() // SHARE
    rows = []
    for comp in range(3):
        whole = None
        for k in range(4):
            turned = (SHARE * (k - comp)) % LANES
            moved = pltpu.roll(came[k], turned, 1) if turned else came[k]
            whole = moved if whole is None else jnp.where(wide == k, moved, whole)
        rows.append(whole)
    left = jnp.concatenate(split_three(jnp.concatenate(rows, axis=0)), axis=0)
    found = jnp.dot(left, send_marks[...], preferred_element_type=jnp.float32)
    height = 3 * SUBS
    found = found[:height] + found[height : 2 * height] + found[2 * height :]
    found = found + own[...]
    for comp in range(3):
        gradient[comp] = found[comp * SUBS : comp * SUBS + TRIALS]
    total = jnp.sum(back[...], axis=0)
    total = jnp.broadcast_to(total[:, LANES - 1 :], (TRIALS, LANES))
    total = jnp.sum(jnp.where(lane == sub, total, 0.0), axis=0, keepdims=True)
    energy_out[...] = total[:, :TRIALS] / 3.0 / elem_total
    low_out[...] = low[:, :TRIALS]


def exchanged(tile, axis):
    count = lax.axis_size(axis)
    near = lax.ppermute(tile, axis, [(i, i ^ 1) for i in range(count)])
    far = lax.ppermute(
        tile, axis, [(i, (i + 1 if i % 2 else i - 1) % count) for i in range(count)]
    )
    return near, far


def per_device(coords, direction, connect, shape_inv, weight, send_node, recv_slot):
    doms, subs = lax.axis_size("dom"), lax.axis_size("sub")
    count = doms * subs
    owned = coords.shape[1]
    elems = connect.shape[1]
    blocks = elems // (2 * LANES)
    local = owned + recv_slot.shape[1]
    f32, i32 = jnp.float32, jnp.int32
    shaped = jax.ShapeDtypeStruct
    params = pltpu.CompilerParams(vmem_limit_bytes=32 * 1024 * 1024)
    hbm = pl.BlockSpec(memory_space=pltpu.HBM)

    def pinned(*arrays):
        return [pltpu.with_memory_space_constraint(x, pltpu.HBM) for x in arrays]

    outgoing, table, sends, slots, connect = pl.pallas_call(
        send_kernel,
        in_specs=[hbm] * 5,
        out_shape=(
            shaped((SUBS, LANES), f32),
            shaped((SUBS, owned), f32),
            shaped(send_node.shape, i32),
            shaped(recv_slot.shape, i32),
            shaped(connect.shape, i32),
        ),
        scratch_shapes=[
            pltpu.VMEM(coords.shape, f32),
            pltpu.VMEM(direction.shape, f32),
            pltpu.SemaphoreType.DMA((5,)),
        ],
        compiler_params=params,
        name="outgoing_nodes",
    )(*pinned(coords, direction, send_node, recv_slot, connect))
    index, corners, inverse, heavy, spots, send_marks = pl.pallas_call(
        functools.partial(prepare_kernel, blocks),
        in_specs=[pl.BlockSpec(memory_space=pltpu.VMEM)] * 4 + [hbm] * 2,
        out_shape=(
            shaped((4, SUBS, elems // 2), i32),
            shaped((12, SUBS, elems // 2), f32),
            shaped((9, SUBS, elems // 2), f32),
            shaped((SUBS, elems // 2), f32),
            shaped((2, 2 * elems, local), jnp.bfloat16),
            shaped((LANES, owned), jnp.bfloat16),
        ),
        scratch_shapes=[
            pltpu.VMEM(shape_inv.shape, f32),
            pltpu.VMEM((elems // LANES, LANES), f32),
            pltpu.SemaphoreType.DMA((2,)),
        ],
        compiler_params=params,
        cost_estimate=pl.CostEstimate(flops=1000000, bytes_accessed=4000000, transcendentals=0),
        name="prepared_elements",
    )(
        table, sends, slots, connect,
        *pinned(shape_inv, weight.reshape(elems // LANES, LANES)),
    )
    near_dom, far_dom = exchanged(outgoing, "dom")
    near_sub, far_sub = exchanged(outgoing, "sub")
    lows, jac = pl.pallas_call(
        functools.partial(det_kernel, blocks, owned),
        out_shape=(
            shaped((count, LANES), f32),
            shaped((9, SUBS, elems // 2), f32),
        ),
        scratch_shapes=[pltpu.VMEM((SUBS, LANES), f32)],
        compiler_params=params,
        name="jacobian_dets",
    )(corners, near_sub, near_dom, far_sub, far_dom, index, inverse)
    lows = lax.all_to_all(lows.reshape(count, 1, LANES), AXES, 0, 0).reshape(count, LANES)
    own, back, low = pl.pallas_call(
        functools.partial(grad_kernel, blocks, subs, doms),
        out_shape=(
            shaped((3 * SUBS, owned), f32),
            shaped((count, TRIALS, LANES), f32),
            shaped((1, LANES), f32),
        ),
        compiler_params=params,
        name="element_gradients",
    )(lows, jac, heavy, spots, inverse)
    back = lax.all_to_all(back, AXES, 0, 0)
    gradient, energy, lowest = pl.pallas_call(
        functools.partial(final_kernel, subs, doms, float(elems * count)),
        out_shape=(
            shaped((3, TRIALS, owned), f32),
            shaped((1, TRIALS), f32),
            shaped((1, TRIALS), f32),
        ),
        compiler_params=params,
        name="owner_sums",
    )(back, own, send_marks, low)
    return gradient.transpose(1, 0, 2), energy.reshape(TRIALS), lowest.reshape(TRIALS)


def solution(mesh):
    placed = (
        P(None, AXES),
        P(None, AXES),
        P(None, AXES),
        P(None, AXES),
        P(AXES),
        P(AXES, None),
        P(AXES, None),
    )
    return jax.shard_map(
        per_device,
        mesh=mesh,
        in_specs=placed,
        out_specs=(P(None, None, AXES), P(), P()),
        check_vma=False,
    )
```

```python
import functools

import jax
import jax.numpy as jnp
from jax import lax
from jax.experimental import pallas as pl
from jax.experimental.pallas import tpu as pltpu
from jax.sharding import PartitionSpec as P

TRIALS = 4
AXES = ("dom", "sub")
LANES = 128
SHARE = 32
SUBS = 8


def lane_ids():
    return lax.broadcasted_iota(jnp.int32, (SUBS, LANES), 1)


def sub_ids():
    return lax.broadcasted_iota(jnp.int32, (SUBS, LANES), 0)


def spread(row):
    return jnp.broadcast_to(row, (SUBS, LANES))


def picked(table, index):
    return jnp.take_along_axis(table, index, axis=1, mode="promise_in_bounds")


def step_lengths():
    trial = sub_ids() & (TRIALS - 1)
    return jnp.where(
        trial == 0, 1.0, jnp.where(trial == 1, 0.5, jnp.where(trial == 2, 0.25, 0.125))
    ).astype(jnp.float32)


def trial_places(table, tile, steps):
    cut = slice(tile * LANES, (tile + 1) * LANES)
    return [
        spread(table[comp : comp + 1, cut]) + steps * spread(table[3 + comp : 4 + comp, cut])
        for comp in range(3)
    ]


def halves(ref, row, block, blocks):
    first = spread(ref[row : row + 1, block * LANES : (block + 1) * LANES])
    later = blocks + block
    second = spread(ref[row : row + 1, later * LANES : (later + 1) * LANES])
    return jnp.where(sub_ids() < TRIALS, first, second)


def split_three(value):
    high = value.astype(jnp.bfloat16)
    rest = value - high.astype(jnp.float32)
    mid = rest.astype(jnp.bfloat16)
    low = (rest - mid.astype(jnp.float32)).astype(jnp.bfloat16)
    return [high, mid, low]


def marks(row, count):
    places = lax.broadcasted_iota(jnp.int32, (count, row.shape[1]), 0)
    hit = places == jnp.broadcast_to(row, (count, row.shape[1]))
    return jnp.where(hit, 1.0, 0.0).astype(jnp.bfloat16)


def column_marks(column, count):
    shape = (column.shape[0], count)
    places = lax.broadcasted_iota(jnp.int32, shape, 1)
    hit = places == jnp.broadcast_to(column, shape)
    return jnp.where(hit, 1.0, 0.0).astype(jnp.bfloat16)


def by_marks(left, right):
    return lax.dot_general(
        left, right, (((1,), (1,)), ((), ())), preferred_element_type=jnp.float32
    )


def fetch(pairs, arrived):
    copies = [
        pltpu.make_async_copy(src, dst, arrived.at[i]) for i, (src, dst) in enumerate(pairs)
    ]
    for copy in copies:
        copy.start()
    return copies


def send_kernel(
    coords, direction, send, slots, connect,
    out, table, send_out, slots_out, connect_out, coords_in, direction_in, arrived,
):
    copies = fetch(
        (
            (coords, coords_in),
            (direction, direction_in),
            (send, send_out),
            (slots, slots_out),
            (connect, connect_out),
        ),
        arrived,
    )
    table[...] = jnp.zeros_like(table)
    for copy in copies[:3]:
        copy.wait()
    table[0:3, :] = coords_in[...]
    table[3:6, :] = direction_in[...]
    index = spread(send_out[...])
    low = index & (LANES - 1)
    first = picked(table[:, :LANES], low)
    second = picked(table[:, LANES:], low)
    out[...] = jnp.where(index < LANES, first, second)
    for copy in copies[3:]:
        copy.wait()


def prepare_kernel(
    blocks, table, sends, slots_in, connect_in, inverse, weight,
    index_out, corner_out, inverse_out, weight_out, marks_out, send_marks_out,
    inverse_in, weight_in, arrived,
):
    copies = fetch(((weight, weight_in), (inverse, inverse_in)), arrived)
    steps = step_lengths()
    firsts, seconds = trial_places(table, 0, steps), trial_places(table, 1, steps)
    owned = table.shape[1]
    nodes = marks_out.shape[2]
    order = marks(slots_in[...], LANES)
    entry = lax.broadcasted_iota(jnp.int32, (16, LANES), 1).astype(jnp.bfloat16)
    came_at = by_marks(entry, order)[:SUBS].astype(jnp.int32)

    def renumbered(given):
        moved = owned + picked(came_at, given & (LANES - 1))
        return jnp.where(given < owned, given, moved)

    for block in range(blocks):
        cut = slice(block * LANES, (block + 1) * LANES)
        for corner in range(4):
            index = halves(connect_in, corner, block, blocks)
            low = index & (LANES - 1)
            for comp in range(3):
                corner_out[3 * corner + comp, :, cut] = jnp.where(
                    index < LANES, picked(firsts[comp], low), picked(seconds[comp], low)
                )
            index_out[corner, :, cut] = renumbered(index)
    columns = jnp.transpose(spread(sends[...]))
    send_marks_out[...] = column_marks(columns[:, :1], send_marks_out.shape[1])
    for block in range(2 * blocks):
        given = connect_in[:, block * LANES : (block + 1) * LANES]
        columns = jnp.transpose(renumbered(jnp.concatenate([given, given], axis=0)))
        half, place = block // blocks, block % blocks
        for corner in range(4):
            row = (4 * place + corner) * LANES
            marks_out[half, row : row + LANES, :] = column_marks(
                columns[:, corner : corner + 1], nodes
            )
    for copy in copies:
        copy.wait()
    for block in range(blocks):
        cut = slice(block * LANES, (block + 1) * LANES)
        weight_out[:, cut] = jnp.where(
            sub_ids() < TRIALS,
            spread(weight_in[block : block + 1, :]),
            spread(weight_in[blocks + block : blocks + block + 1, :]),
        )
        for row in range(9):
            inverse_out[row, :, cut] = halves(inverse_in, row, block, blocks)


def cofactor(m):
    return [
        [
            m[1][1] * m[2][2] - m[1][2] * m[2][1],
            m[1][2] * m[2][0] - m[1][0] * m[2][2],
            m[1][0] * m[2][1] - m[1][1] * m[2][0],
        ],
        [
            m[0][2] * m[2][1] - m[0][1] * m[2][2],
            m[0][0] * m[2][2] - m[0][2] * m[2][0],
            m[0][1] * m[2][0] - m[0][0] * m[2][1],
        ],
        [
            m[0][1] * m[1][2] - m[0][2] * m[1][1],
            m[0][2] * m[1][0] - m[0][0] * m[1][2],
            m[0][0] * m[1][1] - m[0][1] * m[1][0],
        ],
    ]


def det_kernel(
    blocks, owned, orders, corner_in, came3, came2, came1, came0, connect, inverse,
    low_out, jac_out, table,
):
    came = (came0, came1, came2, came3)
    near_dom, far_dom, near_sub, far_sub = (
        tile_of(kind, orders, came) for kind in ("near_dom", "far_dom", "near_sub", "far_sub")
    )
    lane = lane_ids()
    group = lane // SHARE
    from_before = group & 1
    table[...] = jnp.where(
        group < 2,
        jnp.where(from_before != (lax.axis_index("dom") & 1), near_dom, far_dom),
        jnp.where(from_before != (lax.axis_index("sub") & 1), near_sub, far_sub),
    )
    ghosts = trial_places(table, 0, step_lengths())
    lowest = None
    for block in range(blocks):
        cut = slice(block * LANES, (block + 1) * LANES)
        corners = []
        for corner in range(4):
            index = connect[corner, :, cut]
            low = index & (LANES - 1)
            corners.append(
                [
                    jnp.where(
                        index < owned,
                        corner_in[3 * corner + comp, :, cut],
                        picked(ghosts[comp], low),
                    )
                    for comp in range(3)
                ]
            )
        weights = [inverse[row, :, cut] for row in range(9)]
        jac = []
        for comp in range(3):
            edges = [corners[k][comp] - corners[0][comp] for k in (1, 2, 3)]
            jac.append(
                [
                    edges[0] * weights[col]
                    + edges[1] * weights[3 + col]
                    + edges[2] * weights[6 + col]
                    for col in range(3)
                ]
            )
        cofac = cofactor(jac)
        det = jac[0][0] * cofac[0][0] + jac[0][1] * cofac[0][1] + jac[0][2] * cofac[0][2]
        lowest = det if lowest is None else jnp.minimum(lowest, det)
        for comp in range(3):
            for col in range(3):
                jac_out[3 * comp + col, :, cut] = jac[comp][col]
    least = spread_lanes(jnp.min(lowest, axis=1, keepdims=True))
    at_trial = jnp.where(lane == (sub_ids() & (TRIALS - 1)), least, jnp.inf)
    row = jnp.min(at_trial, axis=0, keepdims=True)
    low_out[...] = jnp.broadcast_to(row, low_out.shape)


def spread_lanes(column):
    return jnp.broadcast_to(column, (SUBS, LANES))


def grad_kernel(
    blocks, sub_count, dom_count, lows, jac_in, weight, spots, inverse,
    own_out, back_out, low_out,
):
    lane, sub = lane_ids(), sub_ids()
    lowest_row = jnp.min(lows[...], axis=0, keepdims=True)
    low_out[...] = lowest_row
    lowest = picked(spread(lowest_row), sub & (TRIALS - 1))
    shift = lowest - 1.0 - jnp.abs(lowest)
    energy = None
    sums = [None, None]
    for block in range(blocks):
        cut = slice(block * LANES, (block + 1) * LANES)
        jac = [[jac_in[3 * comp + col, :, cut] for col in range(3)] for comp in range(3)]
        cofac = cofactor(jac)
        det = jac[0][0] * cofac[0][0] + jac[0][1] * cofac[0][1] + jac[0][2] * cofac[0][2]
        squares = jac[0][0] * jac[0][0]
        for comp in range(3):
            for col in range(3):
                if comp + col > 0:
                    squares = squares + jac[comp][col] * jac[comp][col]
        lifted = det - shift
        power = jnp.exp(jnp.log(lifted) * (-2.0 / 3.0))
        heavy = weight[:, cut]
        scaled = heavy * power
        part = scaled * squares
        energy = part if energy is None else energy + part
        scale_jac = scaled * (2.0 / 3.0)
        scale_cof = part / lifted * (2.0 / 9.0)
        weights = [inverse[row, :, cut] for row in range(9)]
        terms = []
        for comp in range(3):
            djac = [scale_jac * jac[comp][col] - scale_cof * cofac[comp][col] for col in range(3)]
            edges = [
                djac[0] * weights[3 * k] + djac[1] * weights[3 * k + 1] + djac[2] * weights[3 * k + 2]
                for k in range(3)
            ]
            terms.append([-(edges[0] + edges[1] + edges[2]), *edges])
        values = jnp.concatenate([jnp.concatenate(parts, axis=1) for parts in terms], axis=0)
        left = jnp.concatenate(split_three(values), axis=0)
        height = 4 * LANES
        for half in range(2):
            right = spots[half, block * height : (block + 1) * height, :]
            found = jnp.dot(left, right, preferred_element_type=jnp.float32)
            sums[half] = found if block == 0 else sums[half] + found
    local = own_out.shape[1] + LANES
    rows = 3 * SUBS
    sums = [s[:rows] + s[rows : 2 * rows] + s[2 * rows :] for s in sums]
    upper = lax.broadcasted_iota(jnp.int32, (SUBS, local), 0) < TRIALS
    ghosts = []
    for comp in range(3):
        cut = slice(comp * SUBS, (comp + 1) * SUBS)
        mixed = jnp.where(upper, sums[0][cut], sums[1][cut])
        both = mixed + pltpu.roll(mixed, TRIALS, 0)
        own_out[cut, :] = both[:, : local - LANES]
        ghosts.append(both[:, local - LANES :])
    energy = spread_lanes(jnp.sum(energy, axis=1, keepdims=True))
    energy = energy + pltpu.roll(energy, TRIALS, 0)
    back_out[...] = jnp.broadcast_to(energy[None, :TRIALS], back_out.shape)
    dom, part = lax.axis_index("dom"), lax.axis_index("sub")
    targets = (
        lax.rem(dom + dom_count - 1, dom_count) * sub_count + part,
        lax.rem(dom + 1, dom_count) * sub_count + part,
        dom * sub_count + lax.rem(part + sub_count - 1, sub_count),
        dom * sub_count + lax.rem(part + 1, sub_count),
    )
    group = lane // SHARE
    for k in range(4):
        tile = energy
        for comp in range(3):
            turned = (SHARE * (comp - k)) % LANES
            moved = pltpu.roll(ghosts[comp], turned, 1) if turned else ghosts[comp]
            tile = jnp.where(group == comp, moved, tile)
        back_out[targets[k]] = tile[:TRIALS]


def final_kernel(
    sub_count, dom_count, elem_total, back, own, send_marks, low, gradient, energy_out, low_out
):
    lane = lane_ids()[:TRIALS]
    sub = sub_ids()[:TRIALS]
    group = lane // SHARE
    dom, part = lax.axis_index("dom"), lax.axis_index("sub")
    sources = (
        lax.rem(dom + 1, dom_count) * sub_count + part,
        lax.rem(dom + dom_count - 1, dom_count) * sub_count + part,
        dom * sub_count + lax.rem(part + 1, sub_count),
        dom * sub_count + lax.rem(part + sub_count - 1, sub_count),
    )
    came = [back[sources[k]] for k in range(4)]
    came = [jnp.concatenate([tile, tile], axis=0) for tile in came]
    wide = lane_ids() // SHARE
    rows = []
    for comp in range(3):
        whole = None
        for k in range(4):
            turned = (SHARE * (k - comp)) % LANES
            moved = pltpu.roll(came[k], turned, 1) if turned else came[k]
            whole = moved if whole is None else jnp.where(wide == k, moved, whole)
        rows.append(whole)
    left = jnp.concatenate(split_three(jnp.concatenate(rows, axis=0)), axis=0)
    found = jnp.dot(left, send_marks[...], preferred_element_type=jnp.float32)
    height = 3 * SUBS
    found = found[:height] + found[height : 2 * height] + found[2 * height :]
    found = found + own[...]
    for comp in range(3):
        gradient[comp] = found[comp * SUBS : comp * SUBS + TRIALS]
    total = jnp.sum(back[...], axis=0)
    total = jnp.broadcast_to(total[:, LANES - 1 :], (TRIALS, LANES))
    total = jnp.sum(jnp.where(lane == sub, total, 0.0), axis=0, keepdims=True)
    energy_out[...] = total[:, :TRIALS] / 3.0 / elem_total
    low_out[...] = low[:, :TRIALS]


def partner(kind, doms, subs, dom, sub):
    if kind == "near_dom":
        return (dom ^ 1) * subs + sub
    if kind == "far_dom":
        return ((dom + 1 if dom % 2 else dom - 1) % doms) * subs + sub
    if kind == "near_sub":
        return dom * subs + (sub ^ 1)
    return dom * subs + (sub + 1 if sub % 2 else sub - 1) % subs


KINDS = {"f": "far_dom", "n": "near_dom", "s": "far_sub", "c": "near_sub"}
FIRST_ORDERS = ("fsnc", "nsfc", "csnf", "csfn")
LAST_ORDERS = ("nsfc", "fsnc", "fscn", "nscf")


def exchanges(subs):
    ends = len(FIRST_ORDERS) + len(LAST_ORDERS)
    if subs < ends:
        orders = ("fsnc",) * subs
    else:
        orders = FIRST_ORDERS + ("fsnc",) * (subs - ends) + LAST_ORDERS
    return [tuple(KINDS[letter] for letter in order) for order in orders]


def exchanged(tile, doms, subs):
    orders = exchanges(subs)
    return [
        lax.ppermute(
            tile,
            AXES,
            [
                (dom * subs + sub, partner(orders[sub][step], doms, subs, dom, sub))
                for dom in range(doms)
                for sub in range(subs)
            ],
        )
        for step in range(4)
    ]


def tile_of(kind, orders, came):
    sub = lax.axis_index("sub")
    tile = None
    for step in range(4):
        places = [place for place, order in enumerate(orders) if order[step] == kind]
        if not places:
            continue
        if tile is None:
            tile = came[step][...]
            continue
        here = functools.reduce(jnp.logical_or, [sub == place for place in places])
        tile = jnp.where(here, came[step][...], tile)
    return tile


def per_device(coords, direction, connect, shape_inv, weight, send_node, recv_slot):
    doms, subs = lax.axis_size("dom"), lax.axis_size("sub")
    count = doms * subs
    owned = coords.shape[1]
    elems = connect.shape[1]
    blocks = elems // (2 * LANES)
    local = owned + recv_slot.shape[1]
    f32, i32 = jnp.float32, jnp.int32
    shaped = jax.ShapeDtypeStruct
    params = pltpu.CompilerParams(vmem_limit_bytes=32 * 1024 * 1024)
    hbm = pl.BlockSpec(memory_space=pltpu.HBM)

    def pinned(*arrays):
        return [pltpu.with_memory_space_constraint(x, pltpu.HBM) for x in arrays]

    outgoing, table, sends, slots, connect = pl.pallas_call(
        send_kernel,
        in_specs=[hbm] * 5,
        out_shape=(
            shaped((SUBS, LANES), f32),
            shaped((SUBS, owned), f32),
            shaped(send_node.shape, i32),
            shaped(recv_slot.shape, i32),
            shaped(connect.shape, i32),
        ),
        scratch_shapes=[
            pltpu.VMEM(coords.shape, f32),
            pltpu.VMEM(direction.shape, f32),
            pltpu.SemaphoreType.DMA((5,)),
        ],
        compiler_params=params,
        name="outgoing_nodes",
    )(*pinned(coords, direction, send_node, recv_slot, connect))
    index, corners, inverse, heavy, spots, send_marks = pl.pallas_call(
        functools.partial(prepare_kernel, blocks),
        in_specs=[pl.BlockSpec(memory_space=pltpu.VMEM)] * 4 + [hbm] * 2,
        out_shape=(
            shaped((4, SUBS, elems // 2), i32),
            shaped((12, SUBS, elems // 2), f32),
            shaped((9, SUBS, elems // 2), f32),
            shaped((SUBS, elems // 2), f32),
            shaped((2, 2 * elems, local), jnp.bfloat16),
            shaped((LANES, owned), jnp.bfloat16),
        ),
        scratch_shapes=[
            pltpu.VMEM(shape_inv.shape, f32),
            pltpu.VMEM((elems // LANES, LANES), f32),
            pltpu.SemaphoreType.DMA((2,)),
        ],
        compiler_params=params,
        cost_estimate=pl.CostEstimate(flops=1000000, bytes_accessed=4000000, transcendentals=0),
        name="prepared_elements",
    )(
        table, sends, slots, connect,
        *pinned(shape_inv, weight.reshape(elems // LANES, LANES)),
    )
    came = exchanged(outgoing, doms, subs)
    lows, jac = pl.pallas_call(
        functools.partial(det_kernel, blocks, owned, exchanges(subs)),
        out_shape=(
            shaped((count, LANES), f32),
            shaped((9, SUBS, elems // 2), f32),
        ),
        scratch_shapes=[pltpu.VMEM((SUBS, LANES), f32)],
        compiler_params=params,
        name="jacobian_dets",
    )(corners, *came[::-1], index, inverse)
    lows = lax.all_to_all(lows.reshape(count, 1, LANES), AXES, 0, 0).reshape(count, LANES)
    own, back, low = pl.pallas_call(
        functools.partial(grad_kernel, blocks, subs, doms),
        out_shape=(
            shaped((3 * SUBS, owned), f32),
            shaped((count, TRIALS, LANES), f32),
            shaped((1, LANES), f32),
        ),
        compiler_params=params,
        name="element_gradients",
    )(lows, jac, heavy, spots, inverse)
    back = lax.all_to_all(back, AXES, 0, 0)
    gradient, energy, lowest = pl.pallas_call(
        functools.partial(final_kernel, subs, doms, float(elems * count)),
        out_shape=(
            shaped((3, TRIALS, owned), f32),
            shaped((1, TRIALS), f32),
            shaped((1, TRIALS), f32),
        ),
        compiler_params=params,
        name="owner_sums",
    )(back, own, send_marks, low)
    return gradient.transpose(1, 0, 2), energy.reshape(TRIALS), lowest.reshape(TRIALS)


def solution(mesh):
    placed = (
        P(None, AXES),
        P(None, AXES),
        P(None, AXES),
        P(None, AXES),
        P(AXES),
        P(AXES, None),
        P(AXES, None),
    )
    return jax.shard_map(
        per_device,
        mesh=mesh,
        in_specs=placed,
        out_specs=(P(None, None, AXES), P(), P()),
        check_vma=False,
    )
```

```python
import functools

import jax
import jax.numpy as jnp
from jax import lax
from jax.experimental import pallas as pl
from jax.experimental.pallas import tpu as pltpu
from jax.sharding import PartitionSpec as P

TRIALS = 4
AXES = ("dom", "sub")
LANES = 128
SHARE = 32
SUBS = 8


def lane_ids():
    return lax.broadcasted_iota(jnp.int32, (SUBS, LANES), 1)


def sub_ids():
    return lax.broadcasted_iota(jnp.int32, (SUBS, LANES), 0)


def spread(row):
    return jnp.broadcast_to(row, (SUBS, LANES))


def picked(table, index):
    return jnp.take_along_axis(table, index, axis=1, mode="promise_in_bounds")


def step_lengths():
    trial = sub_ids() & (TRIALS - 1)
    return jnp.where(
        trial == 0, 1.0, jnp.where(trial == 1, 0.5, jnp.where(trial == 2, 0.25, 0.125))
    ).astype(jnp.float32)


def trial_places(table, tile, steps):
    cut = slice(tile * LANES, (tile + 1) * LANES)
    return [
        spread(table[comp : comp + 1, cut]) + steps * spread(table[3 + comp : 4 + comp, cut])
        for comp in range(3)
    ]


def halves(ref, row, block, blocks):
    first = spread(ref[row : row + 1, block * LANES : (block + 1) * LANES])
    later = blocks + block
    second = spread(ref[row : row + 1, later * LANES : (later + 1) * LANES])
    return jnp.where(sub_ids() < TRIALS, first, second)


def split_three(value):
    high = value.astype(jnp.bfloat16).astype(jnp.float32)
    rest = value - high
    mid = rest.astype(jnp.bfloat16).astype(jnp.float32)
    return jnp.concatenate([high, mid, rest - mid], axis=0).astype(jnp.bfloat16)


def marks(row, count):
    places = lax.broadcasted_iota(jnp.int32, (count, row.shape[1]), 0)
    hit = places == jnp.broadcast_to(row, (count, row.shape[1]))
    return jnp.where(hit, 1.0, 0.0).astype(jnp.bfloat16)


def column_marks(column, count):
    shape = (column.shape[0], count)
    places = lax.broadcasted_iota(jnp.int32, shape, 1)
    hit = places == jnp.broadcast_to(column, shape)
    return jnp.where(hit, 1.0, 0.0).astype(jnp.bfloat16)


def by_marks(left, right):
    return lax.dot_general(
        left, right, (((1,), (1,)), ((), ())), preferred_element_type=jnp.float32
    )


def fetch(pairs, arrived):
    copies = [
        pltpu.make_async_copy(src, dst, arrived.at[i]) for i, (src, dst) in enumerate(pairs)
    ]
    for copy in copies:
        copy.start()
    return copies


def send_kernel(
    coords, direction, send, slots, connect,
    out, table, send_out, slots_out, connect_out, coords_in, direction_in, arrived,
):
    copies = fetch(
        (
            (coords, coords_in),
            (direction, direction_in),
            (send, send_out),
            (slots, slots_out),
            (connect, connect_out),
        ),
        arrived,
    )
    table[...] = jnp.zeros_like(table)
    for copy in copies[:3]:
        copy.wait()
    table[0:3, :] = coords_in[...]
    table[3:6, :] = direction_in[...]
    index = spread(send_out[...])
    low = index & (LANES - 1)
    first = picked(table[:, :LANES], low)
    second = picked(table[:, LANES:], low)
    out[...] = jnp.where(index < LANES, first, second)
    for copy in copies[3:]:
        copy.wait()


def prepare_kernel(
    blocks, table, sends, slots_in, connect_in, inverse, weight,
    index_out, corner_out, inverse_out, weight_out, marks_out, send_marks_out,
    inverse_in, weight_in, arrived,
):
    copies = fetch(((weight, weight_in), (inverse, inverse_in)), arrived)
    steps = step_lengths()
    firsts, seconds = trial_places(table, 0, steps), trial_places(table, 1, steps)
    owned = table.shape[1]
    nodes = marks_out.shape[2]
    order = marks(slots_in[...], LANES)
    entry = lax.broadcasted_iota(jnp.int32, (16, LANES), 1).astype(jnp.bfloat16)
    came_at = by_marks(entry, order)[:SUBS].astype(jnp.int32)

    def renumbered(given):
        moved = owned + picked(came_at, given & (LANES - 1))
        return jnp.where(given < owned, given, moved)

    for block in range(blocks):
        cut = slice(block * LANES, (block + 1) * LANES)
        for corner in range(4):
            index = halves(connect_in, corner, block, blocks)
            low = index & (LANES - 1)
            for comp in range(3):
                corner_out[3 * corner + comp, :, cut] = jnp.where(
                    index < LANES, picked(firsts[comp], low), picked(seconds[comp], low)
                )
            index_out[corner, :, cut] = renumbered(index)
    columns = jnp.transpose(spread(sends[...]))
    send_marks_out[...] = column_marks(columns[:, :1], send_marks_out.shape[1])
    for block in range(2 * blocks):
        given = connect_in[:, block * LANES : (block + 1) * LANES]
        columns = jnp.transpose(renumbered(jnp.concatenate([given, given], axis=0)))
        half, place = block // blocks, block % blocks
        for corner in range(4):
            row = (4 * place + corner) * LANES
            marks_out[half, row : row + LANES, :] = column_marks(
                columns[:, corner : corner + 1], nodes
            )
    for copy in copies:
        copy.wait()
    for block in range(blocks):
        cut = slice(block * LANES, (block + 1) * LANES)
        weight_out[:, cut] = jnp.where(
            sub_ids() < TRIALS,
            spread(weight_in[block : block + 1, :]),
            spread(weight_in[blocks + block : blocks + block + 1, :]),
        )
        for row in range(9):
            inverse_out[row, :, cut] = halves(inverse_in, row, block, blocks)


def cofactor(m):
    return [
        [
            m[1][1] * m[2][2] - m[1][2] * m[2][1],
            m[1][2] * m[2][0] - m[1][0] * m[2][2],
            m[1][0] * m[2][1] - m[1][1] * m[2][0],
        ],
        [
            m[0][2] * m[2][1] - m[0][1] * m[2][2],
            m[0][0] * m[2][2] - m[0][2] * m[2][0],
            m[0][1] * m[2][0] - m[0][0] * m[2][1],
        ],
        [
            m[0][1] * m[1][2] - m[0][2] * m[1][1],
            m[0][2] * m[1][0] - m[0][0] * m[1][2],
            m[0][0] * m[1][1] - m[0][1] * m[1][0],
        ],
    ]


def det_kernel(
    blocks, owned, orders, corner_in, came3, came2, came1, came0, connect, inverse,
    low_out, jac_out, table,
):
    came = (came0, came1, came2, came3)
    near_dom, far_dom, near_sub, far_sub = (
        tile_of(kind, orders, came) for kind in ("near_dom", "far_dom", "near_sub", "far_sub")
    )
    lane = lane_ids()
    group = lane // SHARE
    from_before = group & 1
    table[...] = jnp.where(
        group < 2,
        jnp.where(from_before != (lax.axis_index("dom") & 1), near_dom, far_dom),
        jnp.where(from_before != (lax.axis_index("sub") & 1), near_sub, far_sub),
    )
    ghosts = trial_places(table, 0, step_lengths())
    lowest = None
    for block in range(blocks):
        cut = slice(block * LANES, (block + 1) * LANES)
        corners = []
        for corner in range(4):
            index = connect[corner, :, cut]
            low = index & (LANES - 1)
            corners.append(
                [
                    jnp.where(
                        index < owned,
                        corner_in[3 * corner + comp, :, cut],
                        picked(ghosts[comp], low),
                    )
                    for comp in range(3)
                ]
            )
        weights = [inverse[row, :, cut] for row in range(9)]
        jac = []
        for comp in range(3):
            edges = [corners[k][comp] - corners[0][comp] for k in (1, 2, 3)]
            jac.append(
                [
                    edges[0] * weights[col]
                    + edges[1] * weights[3 + col]
                    + edges[2] * weights[6 + col]
                    for col in range(3)
                ]
            )
        cofac = cofactor(jac)
        det = jac[0][0] * cofac[0][0] + jac[0][1] * cofac[0][1] + jac[0][2] * cofac[0][2]
        lowest = det if lowest is None else jnp.minimum(lowest, det)
        for comp in range(3):
            for col in range(3):
                jac_out[3 * comp + col, :, cut] = jac[comp][col]
    least = spread_lanes(jnp.min(lowest, axis=1, keepdims=True))
    at_trial = jnp.where(lane == (sub_ids() & (TRIALS - 1)), least, jnp.inf)
    row = jnp.min(at_trial, axis=0, keepdims=True)
    low_out[...] = jnp.broadcast_to(row, low_out.shape)


def spread_lanes(column):
    return jnp.broadcast_to(column, (SUBS, LANES))


def grad_kernel(
    blocks, sub_count, dom_count, lows, jac_in, weight, spots, inverse,
    own_out, back_out, low_out,
):
    lane, sub = lane_ids(), sub_ids()
    lowest_row = jnp.min(lows[...], axis=0, keepdims=True)
    low_out[...] = lowest_row
    lowest = picked(spread(lowest_row), sub & (TRIALS - 1))
    shift = lowest - 1.0 - jnp.abs(lowest)
    energy = None
    sums = [None, None]
    for block in range(blocks):
        cut = slice(block * LANES, (block + 1) * LANES)
        jac = [[jac_in[3 * comp + col, :, cut] for col in range(3)] for comp in range(3)]
        cofac = cofactor(jac)
        det = jac[0][0] * cofac[0][0] + jac[0][1] * cofac[0][1] + jac[0][2] * cofac[0][2]
        squares = jac[0][0] * jac[0][0]
        for comp in range(3):
            for col in range(3):
                if comp + col > 0:
                    squares = squares + jac[comp][col] * jac[comp][col]
        lifted = det - shift
        power = jnp.exp(jnp.log(lifted) * (-2.0 / 3.0))
        heavy = weight[:, cut]
        scaled = heavy * power
        part = scaled * squares
        energy = part if energy is None else energy + part
        scale_jac = scaled * (2.0 / 3.0)
        scale_cof = part / lifted * (2.0 / 9.0)
        weights = [inverse[row, :, cut] for row in range(9)]
        terms = []
        for comp in range(3):
            djac = [scale_jac * jac[comp][col] - scale_cof * cofac[comp][col] for col in range(3)]
            edges = [
                djac[0] * weights[3 * k] + djac[1] * weights[3 * k + 1] + djac[2] * weights[3 * k + 2]
                for k in range(3)
            ]
            terms.append([-(edges[0] + edges[1] + edges[2]), *edges])
        values = jnp.concatenate([jnp.concatenate(parts, axis=1) for parts in terms], axis=0)
        left = split_three(values)
        height = 4 * LANES
        for half in range(2):
            right = spots[half, block * height : (block + 1) * height, :]
            found = jnp.dot(left, right, preferred_element_type=jnp.float32)
            sums[half] = found if block == 0 else sums[half] + found
    local = own_out.shape[1] + LANES
    rows = 3 * SUBS
    sums = [s[:rows] + s[rows : 2 * rows] + s[2 * rows :] for s in sums]
    upper = lax.broadcasted_iota(jnp.int32, (SUBS, local), 0) < TRIALS
    ghosts = []
    for comp in range(3):
        cut = slice(comp * SUBS, (comp + 1) * SUBS)
        mixed = jnp.where(upper, sums[0][cut], sums[1][cut])
        both = mixed + pltpu.roll(mixed, TRIALS, 0)
        own_out[cut, :] = both[:, : local - LANES]
        ghosts.append(both[:, local - LANES :])
    energy = spread_lanes(jnp.sum(energy, axis=1, keepdims=True))
    energy = energy + pltpu.roll(energy, TRIALS, 0)
    back_out[...] = jnp.broadcast_to(energy[None, :TRIALS], back_out.shape)
    dom, part = lax.axis_index("dom"), lax.axis_index("sub")
    targets = (
        lax.rem(dom + dom_count - 1, dom_count) * sub_count + part,
        lax.rem(dom + 1, dom_count) * sub_count + part,
        dom * sub_count + lax.rem(part + sub_count - 1, sub_count),
        dom * sub_count + lax.rem(part + 1, sub_count),
    )
    group = lane // SHARE
    for k in range(4):
        tile = energy
        for comp in range(3):
            turned = (SHARE * (comp - k)) % LANES
            moved = pltpu.roll(ghosts[comp], turned, 1) if turned else ghosts[comp]
            tile = jnp.where(group == comp, moved, tile)
        back_out[targets[k]] = tile[:TRIALS]


def final_kernel(
    sub_count, dom_count, elem_total, back, own, send_marks, low, gradient, energy_out, low_out
):
    lane = lane_ids()[:TRIALS]
    sub = sub_ids()[:TRIALS]
    group = lane // SHARE
    dom, part = lax.axis_index("dom"), lax.axis_index("sub")
    sources = (
        lax.rem(dom + 1, dom_count) * sub_count + part,
        lax.rem(dom + dom_count - 1, dom_count) * sub_count + part,
        dom * sub_count + lax.rem(part + 1, sub_count),
        dom * sub_count + lax.rem(part + sub_count - 1, sub_count),
    )
    came = [back[sources[k]] for k in range(4)]
    came = [jnp.concatenate([tile, tile], axis=0) for tile in came]
    wide = lane_ids() // SHARE
    rows = []
    for comp in range(3):
        whole = None
        for k in range(4):
            turned = (SHARE * (k - comp)) % LANES
            moved = pltpu.roll(came[k], turned, 1) if turned else came[k]
            whole = moved if whole is None else jnp.where(wide == k, moved, whole)
        rows.append(whole)
    left = split_three(jnp.concatenate(rows, axis=0))
    found = jnp.dot(left, send_marks[...], preferred_element_type=jnp.float32)
    height = 3 * SUBS
    found = found[:height] + found[height : 2 * height] + found[2 * height :]
    found = found + own[...]
    for comp in range(3):
        gradient[comp] = found[comp * SUBS : comp * SUBS + TRIALS]
    total = jnp.sum(back[...], axis=0)
    total = jnp.broadcast_to(total[:, LANES - 1 :], (TRIALS, LANES))
    total = jnp.sum(jnp.where(lane == sub, total, 0.0), axis=0, keepdims=True)
    energy_out[...] = total[:, :TRIALS] / 3.0 / elem_total
    low_out[...] = low[:, :TRIALS]


def partner(kind, doms, subs, dom, sub):
    if kind == "near_dom":
        return (dom ^ 1) * subs + sub
    if kind == "far_dom":
        return ((dom + 1 if dom % 2 else dom - 1) % doms) * subs + sub
    if kind == "near_sub":
        return dom * subs + (sub ^ 1)
    return dom * subs + (sub + 1 if sub % 2 else sub - 1) % subs


KINDS = {"f": "far_dom", "n": "near_dom", "s": "far_sub", "c": "near_sub"}
FIRST_ORDERS = ("fsnc", "nsfc", "csnf", "csfn")
LAST_ORDERS = ("nsfc", "fsnc", "fscn", "nscf")


def exchanges(subs):
    ends = len(FIRST_ORDERS) + len(LAST_ORDERS)
    if subs < ends:
        orders = ("fsnc",) * subs
    else:
        orders = FIRST_ORDERS + ("fsnc",) * (subs - ends) + LAST_ORDERS
    return [tuple(KINDS[letter] for letter in order) for order in orders]


def exchanged(tile, doms, subs):
    orders = exchanges(subs)
    return [
        lax.ppermute(
            tile,
            AXES,
            [
                (dom * subs + sub, partner(orders[sub][step], doms, subs, dom, sub))
                for dom in range(doms)
                for sub in range(subs)
            ],
        )
        for step in range(4)
    ]


def tile_of(kind, orders, came):
    sub = lax.axis_index("sub")
    tile = None
    for step in range(4):
        places = [place for place, order in enumerate(orders) if order[step] == kind]
        if not places:
            continue
        if tile is None:
            tile = came[step][...]
            continue
        here = functools.reduce(jnp.logical_or, [sub == place for place in places])
        tile = jnp.where(here, came[step][...], tile)
    return tile


def per_device(coords, direction, connect, shape_inv, weight, send_node, recv_slot):
    doms, subs = lax.axis_size("dom"), lax.axis_size("sub")
    count = doms * subs
    owned = coords.shape[1]
    elems = connect.shape[1]
    blocks = elems // (2 * LANES)
    local = owned + recv_slot.shape[1]
    f32, i32 = jnp.float32, jnp.int32
    shaped = jax.ShapeDtypeStruct
    params = pltpu.CompilerParams(vmem_limit_bytes=32 * 1024 * 1024)
    hbm = pl.BlockSpec(memory_space=pltpu.HBM)

    def pinned(*arrays):
        return [pltpu.with_memory_space_constraint(x, pltpu.HBM) for x in arrays]

    outgoing, table, sends, slots, connect = pl.pallas_call(
        send_kernel,
        in_specs=[hbm] * 5,
        out_shape=(
            shaped((SUBS, LANES), f32),
            shaped((SUBS, owned), f32),
            shaped(send_node.shape, i32),
            shaped(recv_slot.shape, i32),
            shaped(connect.shape, i32),
        ),
        scratch_shapes=[
            pltpu.VMEM(coords.shape, f32),
            pltpu.VMEM(direction.shape, f32),
            pltpu.SemaphoreType.DMA((5,)),
        ],
        compiler_params=params,
        name="outgoing_nodes",
    )(*pinned(coords, direction, send_node, recv_slot, connect))
    index, corners, inverse, heavy, spots, send_marks = pl.pallas_call(
        functools.partial(prepare_kernel, blocks),
        in_specs=[pl.BlockSpec(memory_space=pltpu.VMEM)] * 4 + [hbm] * 2,
        out_shape=(
            shaped((4, SUBS, elems // 2), i32),
            shaped((12, SUBS, elems // 2), f32),
            shaped((9, SUBS, elems // 2), f32),
            shaped((SUBS, elems // 2), f32),
            shaped((2, 2 * elems, local), jnp.bfloat16),
            shaped((LANES, owned), jnp.bfloat16),
        ),
        scratch_shapes=[
            pltpu.VMEM(shape_inv.shape, f32),
            pltpu.VMEM((elems // LANES, LANES), f32),
            pltpu.SemaphoreType.DMA((2,)),
        ],
        compiler_params=params,
        cost_estimate=pl.CostEstimate(flops=1000000, bytes_accessed=4000000, transcendentals=0),
        name="prepared_elements",
    )(
        table, sends, slots, connect,
        *pinned(shape_inv, weight.reshape(elems // LANES, LANES)),
    )
    came = exchanged(outgoing, doms, subs)
    lows, jac = pl.pallas_call(
        functools.partial(det_kernel, blocks, owned, exchanges(subs)),
        out_shape=(
            shaped((count, LANES), f32),
            shaped((9, SUBS, elems // 2), f32),
        ),
        scratch_shapes=[pltpu.VMEM((SUBS, LANES), f32)],
        compiler_params=params,
        name="jacobian_dets",
    )(corners, *came[::-1], index, inverse)
    lows = lax.all_to_all(lows.reshape(count, 1, LANES), AXES, 0, 0).reshape(count, LANES)
    own, back, low = pl.pallas_call(
        functools.partial(grad_kernel, blocks, subs, doms),
        out_shape=(
            shaped((3 * SUBS, owned), f32),
            shaped((count, TRIALS, LANES), f32),
            shaped((1, LANES), f32),
        ),
        compiler_params=params,
        name="element_gradients",
    )(lows, jac, heavy, spots, inverse)
    back = lax.all_to_all(back, AXES, 0, 0)
    gradient, energy, lowest = pl.pallas_call(
        functools.partial(final_kernel, subs, doms, float(elems * count)),
        out_shape=(
            shaped((3, TRIALS, owned), f32),
            shaped((1, TRIALS), f32),
            shaped((1, TRIALS), f32),
        ),
        compiler_params=params,
        name="owner_sums",
    )(back, own, send_marks, low)
    return gradient.transpose(1, 0, 2), energy.reshape(TRIALS), lowest.reshape(TRIALS)


def solution(mesh):
    placed = (
        P(None, AXES),
        P(None, AXES),
        P(None, AXES),
        P(None, AXES),
        P(AXES),
        P(AXES, None),
        P(AXES, None),
    )
    return jax.shard_map(
        per_device,
        mesh=mesh,
        in_specs=placed,
        out_specs=(P(None, None, AXES), P(), P()),
        check_vma=False,
    )
```
